32 devices in a mesh: smp: 8 (over z, x), col: 2 (over core), slab: 2 (over y).
Axes of the slice: x: 2, y: 2, z: 4, core: 2. Of those that a mesh axis runs over, the one named last changes fastest.
Arguments:
- jacobian: bfloat16 [256, 32, 16384], P('smp', 'slab', 'col'), may hold values from -0.005722046 to 0.005722046
- local_energy: float32 [256], P('smp'), may hold values from -6 to 6
Outputs:
- update: float32 [32, 16384], P('slab', ('col', 'smp'))
The draws below stay inside these ranges and needn't reach their ends.
All inputs are finite; a program needn't handle non-finite values.
Results may differ from the reference program's by a relative error of at most 0.0085.
Values may be sent and summed in bfloat16 or wider, within the bound.
No kernel may reach another device: no remote copies, remote signals or barrier semaphores. Data moves between devices by JAX's collectives and lax.ppermute only.
A program may use at most 192 MiB of HBM per device.

```python
import jax
import jax.numpy as jnp
from jax import lax

SLABS = 32
SLAB_COLS = 16384
NS = 256
PARAMS = 524288


def draw_jacobian(key, part):
    band_width = 16
    groups = NS // band_width + 1
    row_scale = jnp.exp(jax.random.uniform(jax.random.fold_in(key, 7), (NS,)) * jnp.log(10.0))
    sample_ids = jnp.arange(NS, dtype=jnp.int32)

    def one_slab(index):
        slab_key = jax.random.fold_in(key, index + 100)
        keys = jax.random.split(slab_key, 4)
        offsets = jax.random.randint(keys[1], (SLAB_COLS,), 0, band_width)
        group_ids = (sample_ids[:, None] + offsets[None, :]) // band_width
        noise = jnp.clip(jax.random.normal(keys[0], (NS, SLAB_COLS)), -5.0, 5.0)
        shared = jnp.clip(jax.random.normal(keys[2], (groups, SLAB_COLS)), -5.0, 5.0)
        picked = jnp.take_along_axis(shared, group_ids, axis=0)
        position = (index * SLAB_COLS + jnp.arange(SLAB_COLS)).astype(jnp.float32) / (SLABS * SLAB_COLS)
        col_scale = jnp.exp(jax.random.uniform(keys[3], (SLAB_COLS,)) * jnp.log(10.0)) * (1.0 + 2.0 * position)
        values = (noise + picked) * row_scale[:, None] * col_scale[None, :] / (SLABS * SLAB_COLS)
        return values.astype(jnp.bfloat16)
    stacked = lax.map(one_slab, jnp.arange(SLABS, dtype=jnp.int32))
    return jnp.moveaxis(stacked, 0, 1)


def shard_levels(rng, extent, cuts, low, top_value):
    factor_of = 1.0
    for dim, shards_of in cuts:
        draws = jax.random.uniform(jax.random.fold_in(jax.random.fold_in(rng, 6), dim), (shards_of,), jnp.float32, low / len(cuts), top_value / len(cuts))
        factor_of = factor_of * jnp.repeat(jnp.exp(draws), extent[dim] // shards_of).reshape((-1,) + (1,) * (len(extent) - 1 - dim))
    return factor_of


def scatter_about(rng, shape, deviation, bound, cuts=(), kind=jnp.bfloat16):
    gain = shard_levels(rng, shape, cuts, -0.22, 0.18) if cuts else 1.0
    entries = jax.random.normal(rng, shape, jnp.float32) * deviation * gain
    return jnp.minimum(jnp.maximum(entries, -bound), bound).astype(kind)


def setup_inputs(seed: int = 0) -> dict:
    streams_of = jax.random.split(jax.random.key(seed), 3)
    return {
        "jacobian": draw_jacobian(jax.random.fold_in(streams_of[2], 71), 0),
        "local_energy": scatter_about(streams_of[1], (NS,), 1.0, 6.0, ((0, 8),), jnp.float32),
    }


def center_slab(slab):
    values = slab.astype(jnp.float32)
    mean_row = lax.optimization_barrier(jnp.mean(values, axis=0, keepdims=True))
    return ((values - mean_row) / jnp.sqrt(jnp.float32(NS))).astype(jnp.bfloat16)

def reference(jacobian, local_energy):
    eps = (local_energy - jnp.mean(local_energy)) / jnp.sqrt(jnp.float32(NS))
    slabs_first = jnp.moveaxis(jacobian, 1, 0)

    def add_gram(total, slab):
        centered = center_slab(slab)
        return (total + jnp.dot(centered.astype(jnp.float32), centered.T.astype(jnp.float32), preferred_element_type=jnp.float32), None)
    gram, unused = lax.scan(add_gram, jnp.zeros((NS, NS), jnp.float32), slabs_first)
    shift = 0.01 * jnp.trace(gram) / NS
    factor = jnp.linalg.cholesky(gram + shift * jnp.eye(NS, dtype=jnp.float32))
    middle = lax.linalg.triangular_solve(factor, eps[:, None], left_side=True, lower=True)
    coeffs = lax.linalg.triangular_solve(factor, middle, left_side=True, lower=True, transpose_a=True)[:, 0]

    def slab_delta(carry, slab):
        centered = center_slab(slab).astype(jnp.float32)
        return (carry, jnp.dot(coeffs, centered, precision=lax.Precision.HIGHEST))
    unused, delta = lax.scan(slab_delta, jnp.float32(0.0), slabs_first)
    size = jnp.sqrt(jnp.sum(delta * delta))
    limit = 0.3 * jnp.sqrt(jnp.float32(PARAMS))
    return -jnp.minimum(1.0, limit / size) * delta
```

```python
import functools

import jax
import jax.numpy as jnp
from jax import lax
from jax.experimental import pallas as pl
from jax.experimental.pallas import tpu as pltpu
from jax.sharding import PartitionSpec as P

BLOCK = 64
LANES = 128
EXTRA = 16
F32 = jnp.float32
BF16 = jnp.bfloat16
HIGHEST = lax.Precision.HIGHEST
VMEM_LIMIT = 48 * 1024 * 1024


def mm(a, b, ca, cb):
    return lax.dot_general(
        a, b, (((ca,), (cb,)), ((), ())), precision=HIGHEST, preferred_element_type=F32
    )


def call(kernel, out_shape, grid_spec=None, **kw):
    if grid_spec is not None:
        kw["grid_spec"] = grid_spec
    return pl.pallas_call(
        kernel,
        out_shape=out_shape,
        compiler_params=pltpu.CompilerParams(vmem_limit_bytes=VMEM_LIMIT),
        cost_estimate=pl.CostEstimate(flops=0, bytes_accessed=0, transcendentals=0),
        **kw,
    )


def pack_kernel(early, apart, dest, j_ref, sum_ref, dev_ref, *packed):
    del dest
    rows, slabs, width = j_ref.shape
    first = slabs * early
    step = pl.program_id(0)
    x = j_ref[...].astype(F32)
    total = jnp.sum(x, axis=0)
    sum_ref[0] = total
    spread = x - (total * (1.0 / rows))[None]
    spread = jnp.sum(spread * spread, axis=0)

    @pl.when(step == 0)
    def _():
        dev_ref[...] = spread

    @pl.when(step > 0)
    def _():
        dev_ref[...] += spread

    y = jnp.swapaxes(x, 0, 1)
    y1 = y[:, :early].reshape(first, width).astype(BF16)
    y2 = y[:, early:].reshape(slabs * (rows - early), width).astype(BF16)
    if not apart:
        packed[0][0, :first, :] = y1
        packed[0][0, first:, :] = y2
        return
    for k in range(len(packed) // 2):

        @pl.when(step == k)
        def _():
            packed[2 * k][...] = y1
            packed[2 * k + 1][...] = y2


def pack(jacobian, dests, width, early, apart):
    rows, slabs, _ = jacobian.shape
    count = dests.shape[0]
    if apart:
        heights = (slabs * early, slabs * (rows - early)) * count
        shapes = [pltpu.HBM((h, width), BF16) for h in heights]
        specs = [pl.BlockSpec((h, width), lambda i, d: (0, 0)) for h in heights]
    else:
        shapes = [pltpu.HBM((count, slabs * rows, width), BF16)]
        specs = [pl.BlockSpec((1, slabs * rows, width), lambda i, d: (i, 0, 0))]
    return call(
        functools.partial(pack_kernel, early, apart),
        [
            pltpu.HBM((count, slabs, width), F32),
            pltpu.HBM((slabs, width), F32),
        ]
        + shapes,
        pltpu.PrefetchScalarGridSpec(
            num_scalar_prefetch=1,
            grid=(count,),
            in_specs=[pl.BlockSpec((rows, slabs, width), lambda i, d: (0, 0, d[i]))],
            out_specs=[
                pl.BlockSpec((1, slabs, width), lambda i, d: (i, 0, 0)),
                pl.BlockSpec((slabs, width), lambda i, d: (0, 0)),
            ]
            + specs,
        ),
    )(dests, jacobian)


def place(parts, count, scale, source, mean_row, near_ref, far_refs, half, scratch):
    near = parts - len(far_refs)
    for k in range(parts):
        x = near_ref[k] if k < near else far_refs[k - near][...]
        x = x.astype(F32)[half * count : (half + 1) * count]
        at = pl.multiple_of(source[k] * count, 8)
        scratch[pl.ds(at, count), :] = (x - mean_row) * scale


def early_kernel(parts, count, late_total, scale, source, near_ref, *refs):
    far_refs = refs[: parts // 2]
    mean_ref, extra_ref, c_ref, gram_ref, scratch = refs[parts // 2 :]
    step = pl.program_id(0)
    total = count * parts

    @pl.when(step == 0)
    def _():
        gram_ref[...] = jnp.zeros_like(gram_ref)
        gram_ref[total : total + EXTRA, :] = extra_ref[...]

    for half in range(2):
        mean_row = mean_ref[pl.ds(2 * step + half, 1), :]
        place(parts, count, scale, source, mean_row, near_ref, far_refs, half, scratch)
        c = scratch[...].astype(BF16)
        c_ref[half] = c
        gram_ref[:total, late_total:] += lax.dot_general(
            c, c, (((1,), (1,)), ((), ())), preferred_element_type=F32
        )


def late_kernel(parts, count, scale, source, near_ref, *refs):
    far_refs = refs[: parts // 2]
    mean_ref, c1_ref, c2_ref, gram_ref, scratch, total = refs[parts // 2 :]
    step = pl.program_id(0)

    @pl.when(step == 0)
    def _():
        total[...] = jnp.zeros_like(total)

    for half in range(2):
        mean_row = mean_ref[pl.ds(2 * step + half, 1), :]
        place(parts, count, scale, source, mean_row, near_ref, far_refs, half, scratch)
        c = scratch[...].astype(BF16)
        c2_ref[half] = c
        both = jnp.concatenate([c, c1_ref[half]], axis=0)
        total[...] += lax.dot_general(
            both, c, (((1,), (1,)), ((), ())), preferred_element_type=F32
        )

    @pl.when(step == pl.num_programs(0) - 1)
    def _():
        gram_ref[...] = total[...].T


def early_gram(near, far, source, mean, extra, count, late_total, scale):
    parts = 2 * len(far)
    slabs, width = mean.shape
    total = count * parts
    lanes = total + late_total
    return call(
        functools.partial(early_kernel, parts, count, late_total, scale),
        (
            jax.ShapeDtypeStruct((slabs, total, width), BF16),
            jax.ShapeDtypeStruct((total + EXTRA, lanes), F32),
        ),
        pltpu.PrefetchScalarGridSpec(
            num_scalar_prefetch=1,
            grid=(slabs // 2,),
            in_specs=[pl.BlockSpec((parts // 2, 2 * count, width), lambda i, s: (0, i, 0))]
            + [pl.BlockSpec((2 * count, width), lambda i, s: (i, 0))] * len(far)
            + [
                pl.BlockSpec((slabs, width), lambda i, s: (0, 0)),
                pl.BlockSpec((EXTRA, lanes), lambda i, s: (0, 0)),
            ],
            out_specs=[
                pl.BlockSpec((2, total, width), lambda i, s: (i, 0, 0)),
                pl.BlockSpec((total + EXTRA, lanes), lambda i, s: (0, 0)),
            ],
            scratch_shapes=[pltpu.VMEM((total, width), F32)],
        ),
    )(source, near, *far, mean, extra)


def late_gram(near, far, source, mean, c1, count, scale):
    parts = 2 * len(far)
    slabs, width = mean.shape
    total = count * parts
    first = c1.shape[1]
    lanes = total + first

    skip = (near.shape[1] - slabs * count) // (2 * count)
    return call(
        functools.partial(late_kernel, parts, count, scale),
        (
            jax.ShapeDtypeStruct((slabs, total, width), BF16),
            jax.ShapeDtypeStruct((total, lanes), F32),
        ),
        pltpu.PrefetchScalarGridSpec(
            num_scalar_prefetch=1,
            grid=(slabs // 2,),
            in_specs=[pl.BlockSpec((parts // 2, 2 * count, width), lambda i, s: (0, skip + i, 0))]
            + [pl.BlockSpec((2 * count, width), lambda i, s: (i, 0))] * len(far)
            + [
                pl.BlockSpec((slabs, width), lambda i, s: (0, 0)),
                pl.BlockSpec((2, first, width), lambda i, s: (i, 0, 0)),
            ],
            out_specs=[
                pl.BlockSpec((2, total, width), lambda i, s: (i, 0, 0)),
                pl.BlockSpec((total, lanes), lambda i, s: (0, 0)),
            ],
            scratch_shapes=[pltpu.VMEM((total, width), F32), pltpu.VMEM((lanes, total), F32)],
        ),
    )(source, near, *far, mean, c1)


def inverse_factor(block):
    size = block.shape[0]
    lane = lax.broadcasted_iota(jnp.int32, (8, 2 * size), 1)
    sub = lax.broadcasted_iota(jnp.int32, (8, 2 * size), 0)
    wide = jnp.concatenate([block, jnp.zeros_like(block)], axis=1)
    tiles = []
    for t in range(size // 8):
        unit = jnp.where(lane - size == sub + 8 * t, 1.0, 0.0)
        tiles.append(wide[8 * t : 8 * t + 8] + unit)
    for k in range(size):
        t, r = divmod(k, 8)
        row = tiles[t][r : r + 1]
        row = row * (1.0 / row[:, k : k + 1])
        for u in range(t, size // 8):
            column = tiles[u][:, k : k + 1]
            if u == t:
                column = jnp.where(sub[:, :1] > r, column, 0.0)
            tiles[u] = tiles[u] - column * row
    out = []
    for t in range(size // 8):
        pivot = jnp.sum(jnp.where(lane == sub + 8 * t, tiles[t], 0.0), axis=1, keepdims=True)
        out.append((tiles[t] * lax.rsqrt(pivot))[:, size:])
    return jnp.concatenate(out, axis=0)


def factor_kernel(total, late_total, samples, g_ref, x_ref, aux_ref, work):
    lanes = g_ref.shape[1]
    root = float(samples) ** 0.5
    e1 = g_ref[total : total + 8, :]
    energies = e1[0:1]
    mean = jnp.sum(energies, axis=1, keepdims=True) * (1.0 / samples)
    eps = (energies - mean) * (1.0 / root)
    shift = jnp.sum(e1[1:2], axis=1, keepdims=True) * (0.01 / samples / samples)
    n = total // BLOCK
    diag = lax.broadcasted_iota(jnp.int32, (BLOCK, BLOCK), 0) == lax.broadcasted_iota(
        jnp.int32, (BLOCK, BLOCK), 1
    )

    def start(i, j):
        block = g_ref[BLOCK * i : BLOCK * (i + 1), late_total + BLOCK * j : late_total + BLOCK * (j + 1)]
        return jnp.where(diag, block + shift, block) if i == j else block

    work[...] = jnp.zeros_like(work)
    low = {}
    inv = {}
    for j in range(n):
        for i in range(j, n):
            block = start(i, j)
            for k in range(j):
                block = block - mm(low[i, k], low[j, k], 1, 1)
            if i == j:
                inv[j, j] = inverse_factor(block)
            else:
                low[i, j] = mm(block, inv[j, j], 1, 1)
    for i in range(n):
        for j in range(i):
            total_ij = mm(low[i, j], inv[j, j], 1, 0)
            for k in range(j + 1, i):
                total_ij = total_ij + mm(low[i, k], inv[k, j], 1, 0)
            inv[i, j] = -mm(inv[i, i], total_ij, 1, 0)
        for j in range(i + 1):
            at = late_total + BLOCK * j
            work[late_total + BLOCK * i : late_total + BLOCK * (i + 1), at : at + BLOCK] = inv[i, j]
    x_ref[...] = work[...]
    eps_rows = jnp.broadcast_to(eps, (8, lanes))
    z = mm(eps_rows, work[...], 1, 1)
    sub = lax.broadcasted_iota(jnp.int32, (8, lanes), 0)
    aux_ref[...] = jnp.where(
        sub == 0, z, jnp.where(sub == 1, eps_rows, jnp.broadcast_to(shift, (8, lanes)))
    )


def factor(summed, total, late_total, samples):
    lanes = total + late_total
    return call(
        functools.partial(factor_kernel, total, late_total, samples),
        (
            jax.ShapeDtypeStruct((lanes, lanes), F32),
            jax.ShapeDtypeStruct((8, lanes), F32),
        ),
        scratch_shapes=[pltpu.VMEM((lanes, lanes), F32)],
    )(summed)


def solve_kernel(total, late_total, limit, p2_ref, g_ref, x_ref, aux_ref, out_ref):
    lanes = total + late_total
    strip = p2_ref[...]
    aux = aux_ref[...]
    shift = aux[2:3, :1]
    lane = lax.broadcasted_iota(jnp.int32, (late_total, lanes), 1)
    cross = jnp.where(lane >= late_total, strip, 0.0)
    inverse = x_ref[...]
    w = mm(cross, inverse, 1, 1)
    schur = strip[:, :late_total] - mm(w, w, 1, 1)
    n = late_total // BLOCK
    diag = lax.broadcasted_iota(jnp.int32, (BLOCK, BLOCK), 0) == lax.broadcasted_iota(
        jnp.int32, (BLOCK, BLOCK), 1
    )
    low = {}
    inv = {}
    for j in range(n):
        for i in range(j, n):
            block = schur[BLOCK * i : BLOCK * (i + 1), BLOCK * j : BLOCK * (j + 1)]
            for k in range(j):
                block = block - mm(low[i, k], low[j, k], 1, 1)
            if i == j:
                inv[j] = inverse_factor(jnp.where(diag, block + shift, block))
            else:
                low[i, j] = mm(block, inv[j], 1, 1)
    z_row = jnp.broadcast_to(aux[0:1], (8, lanes))
    rhs = jnp.broadcast_to(aux[1:2, :late_total], (8, late_total)) - mm(z_row, w, 1, 1)
    zs = []
    for i in range(n):
        block = rhs[:, BLOCK * i : BLOCK * (i + 1)]
        for k in range(i):
            block = block - mm(zs[k], low[i, k], 1, 1)
        zs.append(mm(block, inv[i], 1, 1))
    xs = [None] * n
    for i in reversed(range(n)):
        block = zs[i]
        for k in range(i + 1, n):
            block = block - mm(xs[k], low[k, i], 1, 0)
        xs[i] = mm(block, inv[i], 1, 0)
    x2 = jnp.concatenate(xs, axis=1) if n > 1 else xs[0]
    x1 = mm(z_row - mm(x2, w, 1, 0), inverse, 1, 0)
    x1_early = x1[:, late_total:]
    by_cross = mm(x2, cross, 1, 0) * 2.0
    early = mm(x1_early, g_ref[:total, :], 1, 0)
    late = mm(x2, strip[:, :late_total], 1, 0)
    size2 = jnp.sum((by_cross + early) * x1, axis=1, keepdims=True) + jnp.sum(
        late * x2, axis=1, keepdims=True
    )
    clip = jnp.minimum(1.0, limit / jnp.sqrt(jnp.maximum(size2, 0.0)))
    out_ref[...] = x1 * -clip
    out_ref[:, :late_total] = x2 * -clip


def solve(p2, summed, inverse, aux, total, late_total, limit):
    lanes = total + late_total
    return call(
        functools.partial(solve_kernel, total, late_total, limit),
        jax.ShapeDtypeStruct((8, lanes), F32),
    )(p2, summed, inverse, aux)


def update_kernel(late_total, x_ref, c1_ref, c2_ref, out_ref):
    x = x_ref[...]
    high = x.astype(BF16)
    rest = x - high.astype(F32)
    mid = rest.astype(BF16)
    low = (rest - mid.astype(F32)).astype(BF16)
    sub = lax.broadcasted_iota(jnp.int32, x.shape, 0)
    split = jnp.where(
        sub == 0, high.astype(F32), jnp.where(sub == 1, mid.astype(F32), low.astype(F32))
    )
    split = jnp.where(sub < 3, split, 0.0).astype(BF16)
    for half in range(c1_ref.shape[0]):
        both = jnp.concatenate([c2_ref[half], c1_ref[half]], axis=0)
        parts = jnp.dot(split, both, preferred_element_type=F32)
        out_ref[half : half + 1, :] = jnp.sum(parts, axis=0, keepdims=True)


def update(x, c1, c2):
    slabs, total, width = c1.shape
    late_total = c2.shape[1]
    lanes = total + late_total
    group = 8
    return call(
        functools.partial(update_kernel, late_total),
        jax.ShapeDtypeStruct((slabs, width), F32),
        pl.GridSpec(
            grid=(slabs // group,),
            in_specs=[
                pl.BlockSpec((8, lanes), lambda i: (0, 0)),
                pl.BlockSpec((group, total, width), lambda i: (i, 0, 0)),
                pl.BlockSpec((group, late_total, width), lambda i: (i, 0, 0)),
            ],
            out_specs=pl.BlockSpec((group, width), lambda i: (i, 0)),
        ),
    )(x, c1, c2)


def xor_pairs(size, bits):
    return [(i, i ^ bits) for i in range(size)]


SWAP = [(0, 1), (1, 0)]


def sum_smp_slab(a, parts):
    b = lax.ppermute(a, "smp", xor_pairs(parts, 1))
    c = lax.ppermute(a, "slab", SWAP)
    d = lax.ppermute(
        a, ("smp", "slab"), [(2 * i + j, 2 * (i ^ 1) + (1 - j)) for i in range(parts) for j in range(2)]
    )
    a = (a + b) + (c + d)
    bit = 2
    while bit < parts:
        b = lax.ppermute(a, "smp", xor_pairs(parts, bit))
        if 2 * bit < parts:
            c = lax.ppermute(a, "smp", xor_pairs(parts, 2 * bit))
            d = lax.ppermute(a, "smp", xor_pairs(parts, 3 * bit))
            a = (a + b) + (c + d)
        else:
            a = a + b
        bit *= 4
    return a


def sum_small(a, parts):
    return sum_smp_slab(a + lax.ppermute(a, "col", SWAP), parts)


def sum_large(a, parts, ties):
    half = a.shape[0] // 2
    core = lax.axis_index("col")
    rounds = [("slab", SWAP)]
    bit = 1
    while bit < parts:
        rounds.append(("smp", xor_pairs(parts, bit)))
        bit *= 2
    mine = lax.dynamic_slice_in_dim(a, core * half, half, 0)
    other = lax.dynamic_slice_in_dim(a, (1 - core) * half, half, 0)
    if ties[0]:
        other, _ = lax.optimization_barrier((other, ties[0]))
    mine = mine + lax.ppermute(other, "col", SWAP)
    for (axis, pairs), tie in zip(rounds, ties[1:]):
        if tie:
            mine, _ = lax.optimization_barrier((mine, tie))
        mine = mine + lax.ppermute(mine, axis, pairs)
    other = lax.ppermute(mine, "col", SWAP)
    first = jnp.where(core == 0, mine, other)
    second = jnp.where(core == 0, other, mine)
    return jnp.concatenate([first, second], axis=0)


def shards(parts, slab_parts, col_parts, jacobian, local_energy):
    rows, slabs, columns = jacobian.shape
    samples = rows * parts
    params = slabs * slab_parts * columns * col_parts
    late = rows // 4
    early = rows - late
    total, late_total = early * parts, late * parts
    scale = 1.0 / float(samples) ** 0.5
    me = lax.axis_index("smp")

    width = columns // parts
    far = list(range(parts // 2, parts))
    base = me - me % (parts // 2)
    halves = [list(range(parts // 2)), list(range(parts // 2, parts))]
    far_sums, far_spread, *far_rows = pack(jacobian, me ^ jnp.array(far, jnp.int32), width, early, True)
    members = base + jnp.arange(parts // 2, dtype=jnp.int32)
    near_sums, near_spread, near_rows = pack(jacobian, members, width, early, False)

    def send(k, a, after=None):
        if after is not None:
            a, _ = lax.optimization_barrier((a, after))
        return lax.ppermute(a, "smp", xor_pairs(parts, k))

    far1 = [send(k, far_rows[2 * i]) for i, k in enumerate(far)]
    near_got = lax.all_to_all(
        near_rows, "smp", split_axis=0, concat_axis=0, axis_index_groups=halves, tiled=True
    )

    sums = jnp.concatenate([near_sums, far_sums], axis=0)
    spread = jnp.sum(near_spread + far_spread)
    swaps = [(me >> b) & 1 for b in range(parts.bit_length() - 2)]
    sums = sums.reshape((2, parts // 2) + sums.shape[1:])
    for b, odd in enumerate(swaps):
        x = sums[0].reshape((parts // 2 >> (b + 1), 2, 1 << b) + sums.shape[2:])
        x = jnp.where(odd == 1, x[:, ::-1], x).reshape(sums.shape[1:])
        sums = jnp.stack([x, sums[1]])
    sums = sums.reshape((parts,) + sums.shape[2:])
    bit, count = 1, rows
    while bit < parts:
        pairs = sums.reshape((sums.shape[0] // 2, 2) + sums.shape[1:])
        mine, other = pairs[:, 0], send(bit, pairs[:, 1])
        gap = mine - other
        spread = spread + jnp.sum(gap * gap) * (0.5 / count)
        sums = mine + other
        bit, count = 2 * bit, 2 * count
    mean = sums[0] * (1.0 / samples)

    lead = jnp.logical_and(lax.axis_index("col") == 0, lax.axis_index("slab") == 0)
    energies = jnp.where(lead, local_energy, 0.0)
    row = lax.dynamic_update_slice(jnp.zeros((samples,), F32), energies[early:], (me * late,))
    row = lax.dynamic_update_slice(row, energies[:early], (late_total + me * early,))
    spread_row = jnp.where(jnp.arange(samples) == 0, spread, 0.0)
    extra = jnp.concatenate(
        [row[None], spread_row[None], jnp.zeros((EXTRA - 2, samples), F32)], axis=0
    )

    source = jnp.concatenate([members, me ^ jnp.array(far, jnp.int32)])
    c1, gram1 = early_gram(near_got, far1, source, mean, extra, early, late_total, scale)

    far2 = [send(k, far_rows[2 * i + 1], far1) for i, k in enumerate(far)]

    rounds = parts.bit_length() + 1
    ties = [[] for _ in range(rounds)]
    for i, block in enumerate(far2):
        ties[i * 4 // len(far2)].append(block)
    summed = sum_large(gram1, parts, ties)
    inverse, aux = factor(summed, total, late_total, samples)

    c1, aux = lax.optimization_barrier((c1, aux))
    c2, gram2 = late_gram(near_got, far2, source, mean, c1, late, scale)
    strip = sum_small(gram2, parts)
    limit = 0.3 * float(params) ** 0.5
    x = solve(strip, summed, inverse, aux, total, late_total, limit)
    return update(x, c1, c2)


def solution(mesh):
    body = functools.partial(shards, mesh.shape["smp"], mesh.shape["slab"], mesh.shape["col"])
    in_specs = (P("smp", "slab", "col"), P("smp"))
    out_specs = P("slab", ("col", "smp"))
    return jax.shard_map(body, mesh=mesh, in_specs=in_specs, out_specs=out_specs, check_vma=False)
```

```python
import functools

import jax
import jax.numpy as jnp
from jax import lax
from jax.experimental import pallas as pl
from jax.experimental.pallas import tpu as pltpu
from jax.sharding import PartitionSpec as P

BLOCK = 64
LANES = 128
EXTRA = 16
CHUNK = 256
F32 = jnp.float32
BF16 = jnp.bfloat16
HIGHEST = lax.Precision.HIGHEST
MIB = 1024 * 1024
SWAP = [(0, 1), (1, 0)]


def mm(a, b, ca, cb):
    return lax.dot_general(
        a, b, (((ca,), (cb,)), ((), ())), precision=HIGHEST, preferred_element_type=F32
    )


def products(a, b):
    return lax.dot_general(a, b, (((1,), (1,)), ((), ())), preferred_element_type=F32)


def call(kernel, out_shape, grid_spec=None, vmem=58, **kw):
    if grid_spec is not None:
        kw["grid_spec"] = grid_spec
    return pl.pallas_call(
        kernel,
        out_shape=out_shape,
        compiler_params=pltpu.CompilerParams(vmem_limit_bytes=vmem * MIB),
        cost_estimate=pl.CostEstimate(flops=0, bytes_accessed=0, transcendentals=0),
        **kw,
    )


def lane_chunks(width):
    size = min(CHUNK, width)
    return [slice(c, c + size) for c in range(0, width, size)]


def pack_kernel(far_count, dest, j_ref, near_ref, *refs):
    far_refs, (buffer, out, in_sems, out_sems) = refs[:far_count], refs[far_count:]
    step = pl.program_id(0)
    count, rows, slabs, width = buffer.shape

    def read(k):
        columns = pl.ds(pl.multiple_of(dest[k] * width, LANES), width)
        return pltpu.make_async_copy(j_ref.at[:, :, columns], buffer.at[k], in_sems.at[k])

    def write(k):
        target = far_refs[k] if k < far_count else near_ref.at[k - far_count]
        return pltpu.make_async_copy(out.at[k], target, out_sems.at[k])

    @pl.when(step == 0)
    def _():
        for k in range(count):
            read(k).start()

    read(step).wait()
    for part in lane_chunks(width):
        x = jnp.swapaxes(buffer[step, :, :, part].astype(F32), 0, 1)
        out[step, :, part] = x.reshape(slabs * rows, x.shape[2]).astype(BF16)
    for k in range(count):

        @pl.when(step == k)
        def _():
            write(k).start()

    @pl.when(step == count - 1)
    def _():
        for k in range(count):
            write(k).wait()


def pack(jacobian, dests, width):
    rows, slabs, _ = jacobian.shape
    count = dests.shape[0]
    far_count = count // 2
    height = slabs * rows
    return call(
        functools.partial(pack_kernel, far_count),
        [pltpu.HBM((far_count, height, width), BF16)]
        + [pltpu.HBM((height, width), BF16)] * far_count,
        pltpu.PrefetchScalarGridSpec(
            num_scalar_prefetch=1,
            grid=(count,),
            in_specs=[pl.BlockSpec(memory_space=pl.ANY)],
            out_specs=[pl.BlockSpec(memory_space=pl.ANY)] * (1 + far_count),
            scratch_shapes=[
                pltpu.VMEM((count, rows, slabs, width), BF16),
                pltpu.VMEM((count, height, width), BF16),
                pltpu.SemaphoreType.DMA((count,)),
                pltpu.SemaphoreType.DMA((count,)),
            ],
        ),
    )(dests, jacobian)


def near_kernel(rows, near_ref, c_ref, base_ref, gram_ref):
    step = pl.program_id(0)
    parts, height, width = near_ref.shape
    total = parts * rows

    @pl.when(step == 0)
    def _():
        gram_ref[...] = jnp.zeros_like(gram_ref)

    for half in range(height // rows):
        slab = pl.ds(half * rows, rows)
        for part in lane_chunks(width):
            sums = 0.0
            for k in range(parts):
                sums = sums + jnp.sum(near_ref[k, slab, part].astype(F32), axis=0, keepdims=True)
            base = sums * (1.0 / total)
            base_ref[half, :, part] = base
            for k in range(parts):
                x = near_ref[k, slab, part].astype(F32) - base
                c_ref[half, k * rows : (k + 1) * rows, part] = x.astype(BF16)
        c = c_ref[half]
        gram_ref[...] += products(c, c)


def near_products(near, slabs):
    parts, height, width = near.shape
    rows = height // slabs
    total = parts * rows
    group = 2
    return call(
        functools.partial(near_kernel, rows),
        (
            jax.ShapeDtypeStruct((slabs, total, width), BF16),
            jax.ShapeDtypeStruct((slabs, 1, width), F32),
            jax.ShapeDtypeStruct((total, total), F32),
        ),
        pl.GridSpec(
            grid=(slabs // group,),
            in_specs=[pl.BlockSpec((parts, group * rows, width), lambda i: (0, i, 0))],
            out_specs=[
                pl.BlockSpec((group, total, width), lambda i: (i, 0, 0)),
                pl.BlockSpec((group, 1, width), lambda i: (i, 0, 0)),
                pl.BlockSpec((total, total), lambda i: (0, 0)),
            ],
        ),
    )(near)


def far_kernel(rows, place, *refs):
    far_count = len(refs) - 12
    far_refs = refs[:far_count]
    cn_ref, base_ref, near_ref, extra_ref, cf_ref, mine_ref, other_ref, blocks, near, gram, acc, sems = refs[
        far_count:
    ]
    step = pl.program_id(0)
    steps = pl.num_programs(0)
    group, total, width = cf_ref.shape

    def copies(i):
        span = pl.ds(pl.multiple_of(i * group * rows, 16), group * rows)
        return [
            pltpu.make_async_copy(far_refs[k].at[span, :], blocks.at[i, place[k]], sems.at[i, k])
            for k in range(far_count)
        ] + [pltpu.make_async_copy(cn_ref.at[pl.ds(i * group, group)], near.at[i], sems.at[i, far_count])]

    @pl.when(step == 0)
    def _():
        acc[...] = jnp.zeros_like(acc)

        @pl.loop(0, steps)
        def _(i):
            for c in copies(i):
                c.start()

    for c in copies(step):
        c.wait()
    for half in range(group):
        for part in lane_chunks(width):
            base = base_ref[half, :, part]
            for k in range(far_count):
                x = blocks[step, k, half * rows : (half + 1) * rows, part].astype(F32) - base
                cf_ref[half, k * rows : (k + 1) * rows, part] = x.astype(BF16)
        c = cf_ref[half]
        acc[:total, :] += products(near[step, half], c)
        acc[total:, :] += products(c, c)

    @pl.when(step == steps - 1)
    def _():
        low = place[far_count] == 0
        cross, far, near_gram = acc[:total, :], acc[total:, :], near_ref[...]
        gram[:total, :] = jnp.where(low, near_gram, far)
        gram[total : 2 * total, :] = jnp.where(low, far, near_gram)
        gram[2 * total : 3 * total, :] = jnp.where(low, cross, cross.T)
        gram[3 * total :, :] = extra_ref[...]
        count = mine_ref.shape[0]
        core = place[far_count + 1]
        mine_ref[...] = gram[pl.ds(pl.multiple_of(core * count, 8), count), :]
        other_ref[...] = gram[pl.ds(pl.multiple_of((1 - core) * count, 8), count), :]


def far_products(far_blocks, place, cn, base, near_gram, extra):
    slabs, total, width = cn.shape
    far_count = len(far_blocks)
    rows = total // far_count
    group = 2
    steps = slabs // group
    height = 3 * total + EXTRA
    share = jax.ShapeDtypeStruct((height // 2, total), F32)
    return call(
        functools.partial(far_kernel, rows),
        (jax.ShapeDtypeStruct((slabs, total, width), BF16), share, share),
        pltpu.PrefetchScalarGridSpec(
            num_scalar_prefetch=1,
            grid=(steps,),
            in_specs=[pl.BlockSpec(memory_space=pl.ANY)] * (far_count + 1)
            + [
                pl.BlockSpec((group, 1, width), lambda i, s: (i, 0, 0)),
                pl.BlockSpec((total, total), lambda i, s: (0, 0)),
                pl.BlockSpec((EXTRA, total), lambda i, s: (0, 0)),
            ],
            out_specs=[
                pl.BlockSpec((group, total, width), lambda i, s: (i, 0, 0)),
                pl.BlockSpec(share.shape, lambda i, s: (0, 0)),
                pl.BlockSpec(share.shape, lambda i, s: (0, 0)),
            ],
            scratch_shapes=[
                pltpu.VMEM((steps, far_count, group * rows, width), BF16),
                pltpu.VMEM((steps, group, total, width), BF16),
                pltpu.VMEM((height, total), F32),
                pltpu.VMEM((2 * total, total), F32),
                pltpu.SemaphoreType.DMA((steps, far_count + 1)),
            ],
        ),
    )(place, *far_blocks, cn, base, near_gram, extra)


def inverse(block):
    size = block.shape[0]
    shape = (8, 2 * size)
    lane = lax.broadcasted_iota(jnp.int32, shape, 1)
    sub = lax.broadcasted_iota(jnp.int32, shape, 0)
    wide = jnp.concatenate([block, jnp.zeros_like(block)], axis=1)
    count = size // 8
    tiles = [
        wide[8 * t : 8 * t + 8] + jnp.where(lane - size == sub + 8 * t, 1.0, 0.0) for t in range(count)
    ]
    scaled = []

    def pair(c0, c1, at):
        a, b, c = c0[0][at : at + 1], c1[0][at : at + 1], c1[0][at + 1 : at + 2]
        d = 1.0 / (a * c - b * b)
        a, b, c = a * d, b * d, c * d
        g0 = [x * c - y * b for x, y in zip(c0, c1)]
        g1 = [y * a - x * b for x, y in zip(c0, c1)]
        g0[0] = jnp.where(sub > at + 1, g0[0], 0.0)
        g1[0] = jnp.where(sub > at + 1, g1[0], 0.0)
        return g0, g1, (a, b, c)

    for t in range(count):
        normal = jnp.zeros(shape, F32)
        for r in (0, 4):
            k = 8 * t + r
            live = tiles[t:]
            cols = [[jnp.broadcast_to(x[:, k + j : k + j + 1], shape) for x in live] for j in range(4)]
            g0, g1, p = pair(cols[0], cols[1], r)
            r0, r1 = live[0][r : r + 1], live[0][r + 1 : r + 2]
            rest = []
            for j in (2, 3):
                u0, u1 = cols[j][0][r : r + 1], cols[j][0][r + 1 : r + 2]
                rest.append([x - (y * u0 + z * u1) for x, y, z in zip(cols[j], g0, g1)])
            live = [x - (y * r0 + z * r1) for x, y, z in zip(live, g0, g1)]
            h0, h1, q = pair(rest[0], rest[1], r + 2)
            r2, r3 = live[0][r + 2 : r + 3], live[0][r + 3 : r + 4]
            tiles[t:] = [x - (y * r2 + z * r3) for x, y, z in zip(live, h0, h1)]
            for at, (x, y), (a, b, c) in ((r, (r0, r1), p), (r + 2, (r2, r3), q)):
                normal = jnp.where(sub == at, x * c - y * b, normal)
                normal = jnp.where(sub == at + 1, y * a - x * b, normal)
        scaled.append(normal)
    w = jnp.concatenate(tiles, axis=0)[:, size:]
    n = jnp.concatenate(scaled, axis=0)[:, size:]
    return mm(w, n, 0, 0)


def solve_kernel(limit, core, mine_ref, other_ref, x_ref, sums, gram):
    count = mine_ref.shape[0]
    sums[pl.ds(pl.multiple_of(core[0] * count, 8), count), :] = mine_ref[...]
    sums[pl.ds(pl.multiple_of((1 - core[0]) * count, 8), count), :] = other_ref[...]
    half = sums.shape[1]
    samples = 2 * half
    low, high = sums[:half, :], sums[half : 2 * half, :]
    cross = sums[2 * half : 3 * half, :]
    turned = cross.T
    inv = 1.0 / samples
    col_low = (jnp.sum(low, axis=1, keepdims=True) + jnp.sum(cross, axis=1, keepdims=True)) * inv
    col_high = (jnp.sum(high, axis=1, keepdims=True) + jnp.sum(turned, axis=1, keepdims=True)) * inv
    row_low = (jnp.sum(low, axis=0, keepdims=True) + jnp.sum(turned, axis=0, keepdims=True)) * inv
    row_high = (jnp.sum(high, axis=0, keepdims=True) + jnp.sum(cross, axis=0, keepdims=True)) * inv
    mean = (jnp.sum(row_low, axis=1, keepdims=True) + jnp.sum(row_high, axis=1, keepdims=True)) * inv
    gram[:half, :half] = (low - col_low - row_low + mean) * inv
    gram[half:, half:] = (high - col_high - row_high + mean) * inv
    gram[half:, :half] = (turned - col_high - row_low + mean) * inv
    gram[:half, half:] = (cross - col_low - row_high + mean) * inv
    n = samples // BLOCK
    spans = [slice(BLOCK * i, BLOCK * (i + 1)) for i in range(n)]
    on = lax.broadcasted_iota(jnp.int32, (BLOCK, BLOCK), 0) == lax.broadcasted_iota(
        jnp.int32, (BLOCK, BLOCK), 1
    )
    diagonal = sum(jnp.where(on, gram[s, s], 0.0) for s in spans)
    diagonal = jnp.sum(diagonal, axis=0, keepdims=True)
    shift = jnp.sum(diagonal, axis=1, keepdims=True) * (0.01 * inv)

    e = sums[3 * half : 3 * half + 8, :]
    energies = jnp.concatenate([e[0:1], e[1:2]], axis=1)
    center = jnp.sum(energies, axis=1, keepdims=True) * inv
    eps = jnp.broadcast_to((energies - center) * (inv**0.5), (8, samples))

    left, factor, solved = {}, {}, []
    for j in range(n):
        for i in range(j, n):
            block = gram[spans[i], spans[j]]
            if i == j:
                block = jnp.where(on, block + shift, block)
            for k in range(j):
                block = block - mm(factor[i, k], left[j, k], 1, 1)
            left[i, j] = block
        diag = inverse(left[j, j])
        for i in range(j + 1, n):
            factor[i, j] = mm(left[i, j], diag, 1, 0)
        z = eps[:, spans[j]]
        for k in range(j):
            z = z - mm(solved[k][0], factor[j, k], 1, 1)
        solved.append((z, mm(z, diag, 1, 0)))
    xs = [w for _, w in solved]
    for i in reversed(range(n)):
        for j in range(i):
            xs[j] = xs[j] - mm(xs[i], factor[i, j], 1, 0)
    x = jnp.concatenate(xs, axis=1)
    x = x - jnp.sum(x, axis=1, keepdims=True) * inv
    size = jnp.sum(mm(x, gram[...], 1, 0) * x, axis=1, keepdims=True)
    clip = jnp.minimum(1.0, limit / jnp.sqrt(jnp.maximum(size, 0.0)))
    x_ref[...] = x * (clip * -(inv**0.5))


def solve(core, mine, other, limit):
    count, half = mine.shape
    samples = 2 * half
    return call(
        functools.partial(solve_kernel, limit),
        jax.ShapeDtypeStruct((8, samples), F32),
        pltpu.PrefetchScalarGridSpec(
            num_scalar_prefetch=1,
            grid=(1,),
            in_specs=[pl.BlockSpec((count, half), lambda i, s: (0, 0))] * 2,
            out_specs=pl.BlockSpec((8, samples), lambda i, s: (0, 0)),
            scratch_shapes=[
                pltpu.VMEM((2 * count, half), F32),
                pltpu.VMEM((samples, samples), F32),
            ],
        ),
    )(core, mine, other)


def update_kernel(high, x_ref, cn_ref, cf_ref, out_ref):
    total = cn_ref.shape[1]
    sub = lax.broadcasted_iota(jnp.int32, (8, total), 0)

    def split(x):
        first = x.astype(BF16).astype(F32)
        rest = x - first
        second = rest.astype(BF16).astype(F32)
        third = rest - second
        x = jnp.where(sub == 0, first, jnp.where(sub == 1, second, third))
        return jnp.where(sub < 3, x, 0.0).astype(BF16)

    low, up = split(x_ref[:, :total]), split(x_ref[:, total:])
    near = jnp.where(high[0] == 1, up.astype(F32), low.astype(F32)).astype(BF16)
    far = jnp.where(high[0] == 1, low.astype(F32), up.astype(F32)).astype(BF16)
    step = pl.program_id(0)
    group = cn_ref.shape[0]
    for slab in range(group):
        y = jnp.dot(near, cn_ref[slab], preferred_element_type=F32)
        y = y + jnp.dot(far, cf_ref[slab], preferred_element_type=F32)
        out_ref[pl.ds(step * group + slab, 1), :] = jnp.sum(y, axis=0, keepdims=True)


def update(x, high, cn, cf):
    slabs, total, width = cn.shape
    group = 4
    return call(
        update_kernel,
        jax.ShapeDtypeStruct((slabs, width), F32),
        pltpu.PrefetchScalarGridSpec(
            num_scalar_prefetch=1,
            grid=(slabs // group,),
            in_specs=[
                pl.BlockSpec((8, 2 * total), lambda i, s: (0, 0)),
                pl.BlockSpec((group, total, width), lambda i, s: (i, 0, 0)),
                pl.BlockSpec((group, total, width), lambda i, s: (i, 0, 0)),
            ],
            out_specs=pl.BlockSpec((slabs, width), lambda i, s: (0, 0)),
        ),
    )(high, x, cn, cf)


def xor_pairs(size, bits):
    return [(i, i ^ bits) for i in range(size)]


def sum_all(mine, other, parts):
    mine = mine + lax.ppermute(other, "col", SWAP)
    mine = mine + lax.ppermute(mine, "slab", SWAP)
    bit = 1
    while bit < parts:
        mine = mine + lax.ppermute(mine, "smp", xor_pairs(parts, bit))
        bit *= 2
    return mine, lax.ppermute(mine, "col", SWAP)


def shards(parts, slab_parts, col_parts, jacobian, local_energy):
    rows, slabs, columns = jacobian.shape
    params = slabs * slab_parts * columns * col_parts
    half = rows * parts // 2
    me = lax.axis_index("smp")
    count = parts // 2
    far = list(range(count, parts))
    high = me // count
    distance = jnp.arange(count, dtype=jnp.int32)
    partners = me ^ (distance + count)
    members = high * count + distance

    near_rows, *far_rows = pack(jacobian, jnp.concatenate([partners, members]), columns // parts)
    near = lax.all_to_all(
        near_rows,
        "smp",
        split_axis=0,
        concat_axis=0,
        axis_index_groups=[list(range(count)), far],
        tiled=True,
    )
    far_blocks = [lax.ppermute(r, "smp", xor_pairs(parts, k)) for k, r in zip(far, far_rows)]

    lead = jnp.logical_and(lax.axis_index("col") == 0, lax.axis_index("slab") == 0)
    energies = jnp.where(lead, local_energy, 0.0)[None]
    extra = lax.dynamic_update_slice(
        jnp.zeros((EXTRA, half), F32), energies, (high, (me % count) * rows)
    )

    cn, base, near_gram = near_products(near, slabs)
    core = lax.axis_index("col")[None]
    place = jnp.concatenate([partners % count, high[None], core])
    cf, mine, other = far_products(far_blocks, place, cn, base, near_gram, extra)
    mine, other = sum_all(mine, other, parts)
    x = solve(core, mine, other, 0.3 * float(params) ** 0.5)
    return update(x, high[None], cn, cf)


def solution(mesh):
    body = functools.partial(shards, mesh.shape["smp"], mesh.shape["slab"], mesh.shape["col"])
    in_specs = (P("smp", "slab", "col"), P("smp"))
    out_specs = P("slab", ("col", "smp"))
    return jax.shard_map(body, mesh=mesh, in_specs=in_specs, out_specs=out_specs, check_vma=False)
```

```python
import functools

import jax
import jax.numpy as jnp
from jax import lax
from jax.experimental import pallas as pl
from jax.experimental.pallas import tpu as pltpu
from jax.sharding import PartitionSpec as P

BLOCK = 64
LANES = 128
EXTRA = 16
TRANSFER_FLOPS = 10**11
CHUNK = 256
F32 = jnp.float32
BF16 = jnp.bfloat16
HIGHEST = lax.Precision.HIGHEST
MIB = 1024 * 1024
SWAP = [(0, 1), (1, 0)]


def mm(a, b, ca, cb):
    return lax.dot_general(
        a, b, (((ca,), (cb,)), ((), ())), precision=HIGHEST, preferred_element_type=F32
    )


def products(a, b):
    return lax.dot_general(a, b, (((1,), (1,)), ((), ())), preferred_element_type=F32)


def call(kernel, out_shape, grid_spec=None, vmem=58, flops=0, **kw):
    if grid_spec is not None:
        kw["grid_spec"] = grid_spec
    return pl.pallas_call(
        kernel,
        out_shape=out_shape,
        compiler_params=pltpu.CompilerParams(vmem_limit_bytes=vmem * MIB),
        cost_estimate=pl.CostEstimate(flops=flops, bytes_accessed=0, transcendentals=0),
        **kw,
    )


def kernel_mib(half):
    return 16 if half <= 128 else 40


def lane_chunks(width):
    size = min(CHUNK, width)
    return [slice(c, c + size) for c in range(0, width, size)]


def pack_kernel(far_count, j_ref, near_ref, *refs):
    far_refs, (buffer, out, in_sems, out_sems) = refs[:far_count], refs[far_count:]
    count, rows, slabs, width = buffer.shape
    me = lax.axis_index("smp")
    high = me // far_count
    dests = [high * far_count + k for k in range(far_count)]
    dests += [me ^ (far_count + k) for k in range(far_count)]

    def read(k):
        columns = pl.ds(pl.multiple_of(dests[k] * width, LANES), width)
        return pltpu.make_async_copy(j_ref.at[:, :, columns], buffer.at[k], in_sems.at[k])

    def write(k):
        return pltpu.make_async_copy(out.at[k], near_ref.at[k], out_sems.at[k])

    for k in range(count):
        read(k).start()
    for k in range(count):
        read(k).wait()
        for part in lane_chunks(width):
            x = jnp.swapaxes(buffer[k, :, :, part].astype(F32), 0, 1)
            x = x.reshape(slabs * rows, x.shape[2]).astype(BF16)
            if k < far_count:
                out[k, :, part] = x
            else:
                far_refs[k - far_count][:, part] = x
        if k < far_count:
            write(k).start()
    for k in range(far_count):
        write(k).wait()


def pack(jacobian, parts):
    rows, slabs, columns = jacobian.shape
    far_count, width = parts // 2, columns // parts
    height = slabs * rows
    return call(
        functools.partial(pack_kernel, far_count),
        [pltpu.HBM((far_count, height, width), BF16)]
        + [jax.ShapeDtypeStruct((height, width), BF16)] * far_count,
        pl.GridSpec(
            grid=(),
            in_specs=[pl.BlockSpec(memory_space=pl.ANY)],
            out_specs=[pl.BlockSpec(memory_space=pl.ANY)]
            + [pl.BlockSpec(memory_space=pltpu.VMEM)] * far_count,
            scratch_shapes=[
                pltpu.VMEM((parts, rows, slabs, width), BF16),
                pltpu.VMEM((far_count, height, width), BF16),
                pltpu.SemaphoreType.DMA((parts,)),
                pltpu.SemaphoreType.DMA((far_count,)),
            ],
        ),
        vmem=52,
    )(jacobian)


def near_kernel(rows, near_ref, c_ref, base_ref, gram_ref):
    step = pl.program_id(0)
    parts, height, width = near_ref.shape
    total = parts * rows

    @pl.when(step == 0)
    def _():
        gram_ref[...] = jnp.zeros_like(gram_ref)

    for half in range(height // rows):
        slab = pl.ds(half * rows, rows)
        for part in lane_chunks(width):
            sums = 0.0
            for k in range(parts):
                sums = sums + jnp.sum(near_ref[k, slab, part].astype(F32), axis=0, keepdims=True)
            base = sums * (1.0 / total)
            base_ref[half, :, part] = base
            for k in range(parts):
                x = near_ref[k, slab, part].astype(F32) - base
                c_ref[half, k * rows : (k + 1) * rows, part] = x.astype(BF16)
        c = c_ref[half]
        gram_ref[...] += products(c, c)


def near_products(near, slabs):
    parts, height, width = near.shape
    rows = height // slabs
    total = parts * rows
    group = 2
    return call(
        functools.partial(near_kernel, rows),
        (
            jax.ShapeDtypeStruct((slabs, total, width), BF16),
            jax.ShapeDtypeStruct((slabs, 1, width), F32),
            jax.ShapeDtypeStruct((total, total), F32),
        ),
        pl.GridSpec(
            grid=(slabs // group,),
            in_specs=[pl.BlockSpec((parts, group * rows, width), lambda i: (0, i, 0))],
            out_specs=[
                pl.BlockSpec((group, total, width), lambda i: (i, 0, 0)),
                pl.BlockSpec((group, 1, width), lambda i: (i, 0, 0)),
                pl.BlockSpec((total, total), lambda i: (0, 0)),
            ],
        ),
        vmem=kernel_mib(total),
    )(near)


def by_distance(x, axis, size, place):
    blocks = x.shape[axis] // size
    bit = 1
    while bit < blocks:
        parts = [lax.slice_in_dim(x, size * (i ^ bit), size * ((i ^ bit) + 1), axis=axis) for i in range(blocks)]
        x = jnp.where((place & bit) > 0, jnp.concatenate(parts, axis=axis), x)
        bit *= 2
    return x


def far_kernel(rows, place, *refs):
    far_refs, (cn_ref, base_ref, near_ref, extra_ref, mine_ref, other_ref, gram, far) = refs[:-8], refs[-8:]
    slabs, total, width = cn_ref.shape

    def add(slab):
        span = slice(slab * rows, (slab + 1) * rows)
        for part in lane_chunks(width):
            base = base_ref[slab, :, part]
            for k, ref in enumerate(far_refs):
                x = ref[span, part].astype(F32) - base
                far[k * rows : (k + 1) * rows, part] = x.astype(BF16)
        c = far[...]
        return products(jnp.concatenate([cn_ref[slab], c], axis=0), c)

    total_products = add(0)
    for slab in range(1, slabs):
        total_products = total_products + add(slab)
    low = place[0] == 0
    products_far = by_distance(total_products, 1, rows, place[2])
    cross, far_far = products_far[:total], by_distance(products_far[total:], 0, rows, place[2])
    near_near = near_ref[...]
    gram[:total, :] = jnp.where(low, near_near, far_far)
    gram[total : 2 * total, :] = jnp.where(low, far_far, near_near)
    gram[2 * total : 3 * total, :] = jnp.where(low, cross, cross.T)
    gram[3 * total :, :] = extra_ref[...]
    count = mine_ref.shape[0]
    mine_ref[...] = gram[pl.ds(pl.multiple_of(place[1] * count, 8), count), :]
    other_ref[...] = gram[pl.ds(pl.multiple_of((1 - place[1]) * count, 8), count), :]


def far_products(far_blocks, place, cn, base, near_gram, extra):
    _, total, width = cn.shape
    rows = total // len(far_blocks)
    height = 3 * total + EXTRA
    share = jax.ShapeDtypeStruct((height // 2, total), F32)
    whole = pl.BlockSpec(memory_space=pltpu.VMEM)
    return call(
        functools.partial(far_kernel, rows),
        (share, share),
        pltpu.PrefetchScalarGridSpec(
            num_scalar_prefetch=1,
            grid=(),
            in_specs=[whole] * (len(far_blocks) + 4),
            out_specs=[whole] * 2,
            scratch_shapes=[
                pltpu.VMEM((height, total), F32),
                pltpu.VMEM((total, width), BF16),
            ],
        ),
        vmem=kernel_mib(total),
    )(place, *far_blocks, cn, base, near_gram, extra)


def energy_kernel(parts, e_ref, out_ref):
    rows = e_ref.shape[1]
    me = lax.axis_index("smp")
    count = parts // 2
    lead = jnp.logical_and(lax.axis_index("col") == 0, lax.axis_index("slab") == 0)
    shape = out_ref.shape
    wide = jnp.concatenate([e_ref[...]] * count, axis=1)
    row = lax.broadcasted_iota(jnp.int32, shape, 0)
    block = lax.broadcasted_iota(jnp.int32, shape, 1) // rows
    mine = jnp.logical_and(row == me // count, block == me % count)
    out_ref[...] = jnp.where(jnp.logical_and(mine, lead), jnp.broadcast_to(wide, shape), 0.0)


def energy_rows(local_energy, parts):
    rows = local_energy.shape[0]
    return call(
        functools.partial(energy_kernel, parts),
        jax.ShapeDtypeStruct((EXTRA, rows * parts // 2), F32),
        vmem=16,
        flops=TRANSFER_FLOPS,
    )(local_energy[None])


def inverse(block):
    size = block.shape[0]
    shape = (8, 2 * size)
    lane = lax.broadcasted_iota(jnp.int32, shape, 1)
    sub = lax.broadcasted_iota(jnp.int32, shape, 0)
    wide = jnp.concatenate([block, jnp.zeros_like(block)], axis=1)
    count = size // 8
    tiles = [
        wide[8 * t : 8 * t + 8] + jnp.where(lane - size == sub + 8 * t, 1.0, 0.0) for t in range(count)
    ]
    scaled = []
    for t in range(count):
        normal = jnp.zeros(shape, F32)
        live = tiles[t:]
        cols = [[jnp.broadcast_to(x[:, 8 * t + j : 8 * t + j + 1], shape) for x in live] for j in range(8)]
        for at in range(0, 8, 2):
            c0, c1 = cols[at], cols[at + 1]
            a, b, c = c0[0][at : at + 1], c1[0][at : at + 1], c1[0][at + 1 : at + 2]
            d = 1.0 / (a * c - b * b)
            g0 = [(x * c - y * b) * d for x, y in zip(c0, c1)]
            g1 = [(y * a - x * b) * d for x, y in zip(c0, c1)]
            g0[0] = jnp.where(sub > at + 1, g0[0], 0.0)
            g1[0] = jnp.where(sub > at + 1, g1[0], 0.0)
            for j in range(at + 2, 8):
                u0, u1 = cols[j][0][at : at + 1], cols[j][0][at + 1 : at + 2]
                cols[j] = [x - (y * u0 + z * u1) for x, y, z in zip(cols[j], g0, g1)]
            r0, r1 = live[0][at : at + 1], live[0][at + 1 : at + 2]
            live = [x - (y * r0 + z * r1) for x, y, z in zip(live, g0, g1)]
            normal = jnp.where(sub == at, (r0 * c - r1 * b) * d, normal)
            normal = jnp.where(sub == at + 1, (r1 * a - r0 * b) * d, normal)
        tiles[t:] = live
        scaled.append(normal)
    w = jnp.concatenate(tiles, axis=0)[:, size:]
    n = jnp.concatenate(scaled, axis=0)[:, size:]
    return mm(w, n, 0, 0)


def solve_kernel(limit, core, mine_ref, other_ref, x_ref, sums, gram):
    count = mine_ref.shape[0]
    sums[pl.ds(pl.multiple_of(core[0] * count, 8), count), :] = mine_ref[...]
    sums[pl.ds(pl.multiple_of((1 - core[0]) * count, 8), count), :] = other_ref[...]
    half = sums.shape[1]
    samples = 2 * half
    low, high = sums[:half, :], sums[half : 2 * half, :]
    cross = sums[2 * half : 3 * half, :]
    turned = cross.T
    inv = 1.0 / samples
    col_low = (jnp.sum(low, axis=1, keepdims=True) + jnp.sum(cross, axis=1, keepdims=True)) * inv
    col_high = (jnp.sum(high, axis=1, keepdims=True) + jnp.sum(turned, axis=1, keepdims=True)) * inv
    row_low = (jnp.sum(low, axis=0, keepdims=True) + jnp.sum(turned, axis=0, keepdims=True)) * inv
    row_high = (jnp.sum(high, axis=0, keepdims=True) + jnp.sum(cross, axis=0, keepdims=True)) * inv
    mean = (jnp.sum(row_low, axis=1, keepdims=True) + jnp.sum(row_high, axis=1, keepdims=True)) * inv
    gram[:half, :half] = (low - col_low - row_low + mean) * inv
    gram[half:, half:] = (high - col_high - row_high + mean) * inv
    gram[half:, :half] = (turned - col_high - row_low + mean) * inv
    gram[:half, half:] = (cross - col_low - row_high + mean) * inv
    n = samples // BLOCK
    spans = [slice(BLOCK * i, BLOCK * (i + 1)) for i in range(n)]
    on = lax.broadcasted_iota(jnp.int32, (BLOCK, BLOCK), 0) == lax.broadcasted_iota(
        jnp.int32, (BLOCK, BLOCK), 1
    )
    diagonal = sum(jnp.where(on, gram[s, s], 0.0) for s in spans)
    diagonal = jnp.sum(diagonal, axis=0, keepdims=True)
    shift = jnp.sum(diagonal, axis=1, keepdims=True) * (0.01 * inv)

    e = sums[3 * half : 3 * half + 8, :]
    energies = jnp.concatenate([e[0:1], e[1:2]], axis=1)
    center = jnp.sum(energies, axis=1, keepdims=True) * inv
    eps = jnp.broadcast_to((energies - center) * (inv**0.5), (8, samples))

    left, factor, solved = {}, {}, []
    for j in range(n):
        for i in range(j, n):
            block = gram[spans[i], spans[j]]
            if i == j:
                block = jnp.where(on, block + shift, block)
            for k in range(j):
                block = block - mm(factor[i, k], left[j, k], 1, 1)
            left[i, j] = block
        diag = inverse(left[j, j])
        for i in range(j + 1, n):
            factor[i, j] = mm(left[i, j], diag, 1, 0)
        z = eps[:, spans[j]]
        for k in range(j):
            z = z - mm(solved[k][0], factor[j, k], 1, 1)
        solved.append((z, mm(z, diag, 1, 0)))
    xs = [w for _, w in solved]
    for i in reversed(range(n)):
        for j in range(i):
            xs[j] = xs[j] - mm(xs[i], factor[i, j], 1, 0)
    x = jnp.concatenate(xs, axis=1)
    x = x - jnp.sum(x, axis=1, keepdims=True) * inv
    size = jnp.sum(mm(x, gram[...], 1, 0) * x, axis=1, keepdims=True)
    clip = jnp.minimum(1.0, limit / jnp.sqrt(jnp.maximum(size, 0.0)))
    x_ref[...] = x * (clip * -(inv**0.5))


def solve(core, mine, other, limit):
    count, half = mine.shape
    samples = 2 * half
    return call(
        functools.partial(solve_kernel, limit),
        jax.ShapeDtypeStruct((8, samples), F32),
        pltpu.PrefetchScalarGridSpec(
            num_scalar_prefetch=1,
            grid=(1,),
            in_specs=[pl.BlockSpec((count, half), lambda i, s: (0, 0))] * 2,
            out_specs=pl.BlockSpec((8, samples), lambda i, s: (0, 0)),
            scratch_shapes=[
                pltpu.VMEM((2 * count, half), F32),
                pltpu.VMEM((samples, samples), F32),
            ],
        ),
        vmem=kernel_mib(half),
    )(core, mine, other)


def update_kernel(rows, place, x_ref, cn_ref, base_ref, *refs):
    far_refs, out_ref = refs[:-1], refs[-1]
    slabs, total, _ = cn_ref.shape
    sub = lax.broadcasted_iota(jnp.int32, (8, total), 0)

    def split(x):
        first = x.astype(BF16).astype(F32)
        rest = x - first
        second = rest.astype(BF16).astype(F32)
        x = jnp.where(sub == 0, first, jnp.where(sub == 1, second, rest - second))
        return jnp.where(sub < 3, x, 0.0).astype(BF16)

    low, high = x_ref[:, :total], x_ref[:, total:]
    is_low = place[0] == 0
    near = jnp.where(is_low, low, high)
    far = by_distance(jnp.where(is_low, high, low), 1, rows, place[2])
    weight = jnp.sum(far[:1], axis=1, keepdims=True)
    both = jnp.concatenate([split(near), split(far)], axis=1)

    def one(slab):
        span = slice(slab * rows, (slab + 1) * rows)
        block = jnp.concatenate([cn_ref[slab]] + [ref[span, :] for ref in far_refs], axis=0)
        y = jnp.dot(both, block, preferred_element_type=F32)
        out_ref[slab : slab + 1, :] = jnp.sum(y, axis=0, keepdims=True) - weight * base_ref[slab]

    for slab in range(slabs):
        one(slab)


def update(x, place, cn, base, far_blocks):
    slabs, total, width = cn.shape
    whole = pl.BlockSpec(memory_space=pltpu.VMEM)
    return call(
        functools.partial(update_kernel, total // len(far_blocks)),
        jax.ShapeDtypeStruct((slabs, width), F32),
        pltpu.PrefetchScalarGridSpec(
            num_scalar_prefetch=1,
            grid=(),
            in_specs=[whole] * (3 + len(far_blocks)),
            out_specs=whole,
        ),
        vmem=kernel_mib(total),
    )(place, x, cn, base, *far_blocks)


def xor_pairs(size, bits):
    return [(i, i ^ bits) for i in range(size)]


def sum_all(mine, other, parts):
    mine = mine + lax.ppermute(other, "col", SWAP)
    mine = mine + lax.ppermute(mine, "slab", SWAP)
    bit = 1
    while bit < parts:
        mine = mine + lax.ppermute(mine, "smp", xor_pairs(parts, bit))
        bit *= 2
    return mine, lax.ppermute(mine, "col", SWAP)


def shards(parts, slab_parts, col_parts, jacobian, local_energy):
    rows, slabs, columns = jacobian.shape
    params = slabs * slab_parts * columns * col_parts
    half = rows * parts // 2
    me = lax.axis_index("smp")
    count = parts // 2
    far = list(range(count, parts))
    high = me // count

    near_rows, *far_rows = pack(jacobian, parts)
    near = lax.all_to_all(
        near_rows,
        "smp",
        split_axis=0,
        concat_axis=0,
        axis_index_groups=[list(range(count)), far],
        tiled=True,
    )
    far_blocks = [lax.ppermute(r, "smp", xor_pairs(parts, k)) for k, r in zip(far, far_rows)]

    extra = energy_rows(local_energy, parts)
    cn, base, near_gram = near_products(near, slabs)
    core = lax.axis_index("col")
    place = jnp.stack([high, core, me % count])
    mine, other = far_products(far_blocks, place, cn, base, near_gram, extra)
    mine, other = sum_all(mine, other, parts)
    x = solve(core[None], mine, other, 0.3 * float(params) ** 0.5)
    return update(x, place, cn, base, far_blocks)


def solution(mesh):
    body = functools.partial(shards, mesh.shape["smp"], mesh.shape["slab"], mesh.shape["col"])
    in_specs = (P("smp", "slab", "col"), P("smp"))
    out_specs = P("slab", ("col", "smp"))
    return jax.shard_map(body, mesh=mesh, in_specs=in_specs, out_specs=out_specs, check_vma=False)
```

```python
import functools

import jax
import jax.numpy as jnp
from jax import lax
from jax.experimental import pallas as pl
from jax.experimental.pallas import tpu as pltpu
from jax.sharding import PartitionSpec as P

BLOCK = 64
LANES = 128
EXTRA = 16
TRANSFER_FLOPS = 10**11
CHUNK = 256
F32 = jnp.float32
BF16 = jnp.bfloat16
HIGHEST = lax.Precision.HIGHEST
MIB = 1024 * 1024
SWAP = [(0, 1), (1, 0)]


def mm(a, b, ca, cb):
    return lax.dot_general(
        a, b, (((ca,), (cb,)), ((), ())), precision=HIGHEST, preferred_element_type=F32
    )


def products(a, b):
    return lax.dot_general(a, b, (((1,), (1,)), ((), ())), preferred_element_type=F32)


def call(kernel, out_shape, grid_spec=None, vmem=58, flops=0, **kw):
    if grid_spec is not None:
        kw["grid_spec"] = grid_spec
    return pl.pallas_call(
        kernel,
        out_shape=out_shape,
        compiler_params=pltpu.CompilerParams(vmem_limit_bytes=vmem * MIB),
        cost_estimate=pl.CostEstimate(flops=flops, bytes_accessed=0, transcendentals=0),
        **kw,
    )


def kernel_mib(half):
    return 16 if half <= 128 else 40


def lane_chunks(width):
    size = min(CHUNK, width)
    return [slice(c, c + size) for c in range(0, width, size)]


def pack_kernel(parts, far, j_ref, *refs):
    half = parts // 2
    out_refs, (buffer, out, in_sems, out_sems) = refs[:-4], refs[-4:]
    count, rows, slabs, width = buffer.shape
    me = lax.axis_index("smp")

    def read(k):
        dest = me ^ far[k] if far else me // half * half + k
        columns = pl.ds(pl.multiple_of(dest * width, LANES), width)
        return pltpu.make_async_copy(j_ref.at[:, :, columns], buffer.at[k], in_sems.at[k])

    def write(k):
        target = out_refs[k] if far else out_refs[0].at[k]
        return pltpu.make_async_copy(out.at[k], target, out_sems.at[k])

    for k in range(count):
        read(k).start()
    for k in range(count):
        read(k).wait()
        for part in lane_chunks(width):
            x = jnp.swapaxes(buffer[k, :, :, part].astype(F32), 0, 1)
            out[k, :, part] = x.reshape(slabs * rows, x.shape[2]).astype(BF16)
        write(k).start()
    for k in range(count):
        write(k).wait()


def pack(jacobian, parts, far):
    rows, slabs, columns = jacobian.shape
    count, width = len(far) or parts // 2, columns // parts
    height = slabs * rows
    shapes = [(height, width)] * count if far else [(count, height, width)]
    return call(
        functools.partial(pack_kernel, parts, far),
        [pltpu.HBM(shape, BF16) for shape in shapes],
        pl.GridSpec(
            grid=(),
            in_specs=[pl.BlockSpec(memory_space=pl.ANY)],
            out_specs=[pl.BlockSpec(memory_space=pl.ANY)] * len(shapes),
            scratch_shapes=[
                pltpu.VMEM((count, rows, slabs, width), BF16),
                pltpu.VMEM((count, height, width), BF16),
                pltpu.SemaphoreType.DMA((count,)),
                pltpu.SemaphoreType.DMA((count,)),
            ],
        ),
        vmem=58,
    )(jacobian)


def near_kernel(rows, near_ref, c_ref, base_ref, gram_ref):
    step = pl.program_id(0)
    parts, height, width = near_ref.shape
    total = parts * rows

    @pl.when(step == 0)
    def _():
        gram_ref[...] = jnp.zeros_like(gram_ref)

    for half in range(height // rows):
        slab = pl.ds(half * rows, rows)
        for part in lane_chunks(width):
            sums = 0.0
            for k in range(parts):
                sums = sums + jnp.sum(near_ref[k, slab, part].astype(F32), axis=0, keepdims=True)
            base = sums * (1.0 / total)
            base_ref[half, :, part] = base
            for k in range(parts):
                x = near_ref[k, slab, part].astype(F32) - base
                c_ref[half, k * rows : (k + 1) * rows, part] = x.astype(BF16)
        c = c_ref[half]
        gram_ref[...] += products(c, c)


def near_products(near, slabs):
    parts, height, width = near.shape
    rows = height // slabs
    total = parts * rows
    group = 2
    return call(
        functools.partial(near_kernel, rows),
        (
            jax.ShapeDtypeStruct((slabs, total, width), BF16),
            jax.ShapeDtypeStruct((slabs, 1, width), F32),
            jax.ShapeDtypeStruct((total, total), F32),
        ),
        pl.GridSpec(
            grid=(slabs // group,),
            in_specs=[pl.BlockSpec((parts, group * rows, width), lambda i: (0, i, 0))],
            out_specs=[
                pl.BlockSpec((group, total, width), lambda i: (i, 0, 0)),
                pl.BlockSpec((group, 1, width), lambda i: (i, 0, 0)),
                pl.BlockSpec((total, total), lambda i: (0, 0)),
            ],
        ),
        vmem=kernel_mib(total),
    )(near)


def by_distance(x, axis, size, place):
    blocks = x.shape[axis] // size
    bit = 1
    while bit < blocks:
        parts = [lax.slice_in_dim(x, size * (i ^ bit), size * ((i ^ bit) + 1), axis=axis) for i in range(blocks)]
        x = jnp.where((place & bit) > 0, jnp.concatenate(parts, axis=axis), x)
        bit *= 2
    return x


def far_kernel(rows, place, *refs):
    far_refs, (cn_ref, base_ref, near_ref, extra_ref, mine_ref, other_ref, gram, far) = refs[:-8], refs[-8:]
    slabs, total, width = cn_ref.shape

    def add(slab):
        span = slice(slab * rows, (slab + 1) * rows)
        for part in lane_chunks(width):
            base = base_ref[slab, :, part]
            for k, ref in enumerate(far_refs):
                x = ref[span, part].astype(F32) - base
                far[k * rows : (k + 1) * rows, part] = x.astype(BF16)
        c = far[...]
        return products(jnp.concatenate([cn_ref[slab], c], axis=0), c)

    total_products = add(0)
    for slab in range(1, slabs):
        total_products = total_products + add(slab)
    low = place[0] == 0
    products_far = by_distance(total_products, 1, rows, place[2])
    cross, far_far = products_far[:total], by_distance(products_far[total:], 0, rows, place[2])
    near_near = near_ref[...]
    low_low = jnp.where(low, near_near, far_far)
    high_high = jnp.where(low, far_far, near_near)
    row = lax.broadcasted_iota(jnp.int32, (total, total), 0)
    lane = lax.broadcasted_iota(jnp.int32, (total, total), 1)
    gram[:total, :] = jnp.where(row >= lane, low_low, high_high)
    gram[total : 2 * total, :] = jnp.where(low, cross, cross.T)
    diagonal = jnp.sum(jnp.where(row == lane, high_high, 0.0), axis=0, keepdims=True)
    gram[2 * total :, :] = jnp.where(row[:EXTRA] == 2, diagonal, extra_ref[...])
    count = mine_ref.shape[0]
    mine_ref[...] = gram[pl.ds(pl.multiple_of(place[1] * count, 8), count), :]
    other_ref[...] = gram[pl.ds(pl.multiple_of((1 - place[1]) * count, 8), count), :]


def far_products(far_blocks, place, cn, base, near_gram, extra):
    _, total, width = cn.shape
    rows = total // len(far_blocks)
    height = 2 * total + EXTRA
    share = jax.ShapeDtypeStruct((height // 2, total), F32)
    whole = pl.BlockSpec(memory_space=pltpu.VMEM)
    return call(
        functools.partial(far_kernel, rows),
        (share, share),
        pltpu.PrefetchScalarGridSpec(
            num_scalar_prefetch=1,
            grid=(),
            in_specs=[whole] * (len(far_blocks) + 4),
            out_specs=[whole] * 2,
            scratch_shapes=[
                pltpu.VMEM((height, total), F32),
                pltpu.VMEM((total, width), BF16),
            ],
        ),
        vmem=kernel_mib(total),
    )(place, *far_blocks, cn, base, near_gram, extra)


def energy_kernel(parts, e_ref, out_ref):
    rows = e_ref.shape[1]
    me = lax.axis_index("smp")
    count = parts // 2
    lead = jnp.logical_and(lax.axis_index("col") == 0, lax.axis_index("slab") == 0)
    shape = out_ref.shape
    wide = jnp.concatenate([e_ref[...]] * count, axis=1)
    row = lax.broadcasted_iota(jnp.int32, shape, 0)
    block = lax.broadcasted_iota(jnp.int32, shape, 1) // rows
    mine = jnp.logical_and(row == me // count, block == me % count)
    out_ref[...] = jnp.where(jnp.logical_and(mine, lead), jnp.broadcast_to(wide, shape), 0.0)


def energy_rows(local_energy, parts):
    rows = local_energy.shape[0]
    return call(
        functools.partial(energy_kernel, parts),
        jax.ShapeDtypeStruct((EXTRA, rows * parts // 2), F32),
        vmem=16,
        flops=TRANSFER_FLOPS,
    )(local_energy[None])


def inverse(block):
    size = block.shape[0]
    shape = (8, 2 * size)
    lane = lax.broadcasted_iota(jnp.int32, shape, 1)
    sub = lax.broadcasted_iota(jnp.int32, shape, 0)
    wide = jnp.concatenate([block, jnp.zeros_like(block)], axis=1)
    count = size // 8
    tiles = [
        wide[8 * t : 8 * t + 8] + jnp.where(lane - size == sub + 8 * t, 1.0, 0.0) for t in range(count)
    ]
    scaled = []
    for t in range(count):
        normal = jnp.zeros(shape, F32)
        live = tiles[t:]
        cols = [[jnp.broadcast_to(x[:, 8 * t + j : 8 * t + j + 1], shape) for x in live] for j in range(8)]
        for at in range(0, 8, 2):
            c0, c1 = cols[at], cols[at + 1]
            a, b, c = c0[0][at : at + 1], c1[0][at : at + 1], c1[0][at + 1 : at + 2]
            d = 1.0 / (a * c - b * b)
            g0 = [(x * c - y * b) * d for x, y in zip(c0, c1)]
            g1 = [(y * a - x * b) * d for x, y in zip(c0, c1)]
            g0[0] = jnp.where(sub > at + 1, g0[0], 0.0)
            g1[0] = jnp.where(sub > at + 1, g1[0], 0.0)
            for j in range(at + 2, 8):
                u0, u1 = cols[j][0][at : at + 1], cols[j][0][at + 1 : at + 2]
                cols[j] = [x - (y * u0 + z * u1) for x, y, z in zip(cols[j], g0, g1)]
            r0, r1 = live[0][at : at + 1], live[0][at + 1 : at + 2]
            live = [x - (y * r0 + z * r1) for x, y, z in zip(live, g0, g1)]
            normal = jnp.where(sub == at, (r0 * c - r1 * b) * d, normal)
            normal = jnp.where(sub == at + 1, (r1 * a - r0 * b) * d, normal)
        tiles[t:] = live
        scaled.append(normal)
    w = jnp.concatenate(tiles, axis=0)[:, size:]
    n = jnp.concatenate(scaled, axis=0)[:, size:]
    return mm(w, n, 0, 0)


def solve_kernel(limit, core, mine_ref, other_ref, x_ref, sums, gram):
    count = mine_ref.shape[0]
    sums[pl.ds(pl.multiple_of(core[0] * count, 8), count), :] = mine_ref[...]
    sums[pl.ds(pl.multiple_of((1 - core[0]) * count, 8), count), :] = other_ref[...]
    half = sums.shape[1]
    samples = 2 * half
    both, cross = sums[:half, :], sums[half : 2 * half, :]
    e = sums[2 * half : 2 * half + 8, :]
    flipped, turned = both.T, cross.T
    row = lax.broadcasted_iota(jnp.int32, (half, half), 0)
    lane = lax.broadcasted_iota(jnp.int32, (half, half), 1)
    low = jnp.where(row >= lane, both, flipped)
    high = jnp.where(row < lane, both, jnp.where(row > lane, flipped, e[2:3]))
    inv = 1.0 / samples
    col_low = (jnp.sum(low, axis=1, keepdims=True) + jnp.sum(cross, axis=1, keepdims=True)) * inv
    col_high = (jnp.sum(high, axis=1, keepdims=True) + jnp.sum(turned, axis=1, keepdims=True)) * inv
    row_low = (jnp.sum(low, axis=0, keepdims=True) + jnp.sum(turned, axis=0, keepdims=True)) * inv
    row_high = (jnp.sum(high, axis=0, keepdims=True) + jnp.sum(cross, axis=0, keepdims=True)) * inv
    mean = (jnp.sum(row_low, axis=1, keepdims=True) + jnp.sum(row_high, axis=1, keepdims=True)) * inv
    gram[:half, :half] = (low - col_low - row_low + mean) * inv
    gram[half:, half:] = (high - col_high - row_high + mean) * inv
    gram[half:, :half] = (turned - col_high - row_low + mean) * inv
    gram[:half, half:] = (cross - col_low - row_high + mean) * inv
    n = samples // BLOCK
    spans = [slice(BLOCK * i, BLOCK * (i + 1)) for i in range(n)]
    on = lax.broadcasted_iota(jnp.int32, (BLOCK, BLOCK), 0) == lax.broadcasted_iota(
        jnp.int32, (BLOCK, BLOCK), 1
    )
    diagonal = sum(jnp.where(on, gram[s, s], 0.0) for s in spans)
    diagonal = jnp.sum(diagonal, axis=0, keepdims=True)
    shift = jnp.sum(diagonal, axis=1, keepdims=True) * (0.01 * inv)

    energies = jnp.concatenate([e[0:1], e[1:2]], axis=1)
    center = jnp.sum(energies, axis=1, keepdims=True) * inv
    eps = jnp.broadcast_to((energies - center) * (inv**0.5), (8, samples))

    left, factor, solved = {}, {}, []
    for j in range(n):
        for i in range(j, n):
            block = gram[spans[i], spans[j]]
            if i == j:
                block = jnp.where(on, block + shift, block)
            for k in range(j):
                block = block - mm(factor[i, k], left[j, k], 1, 1)
            left[i, j] = block
        diag = inverse(left[j, j])
        for i in range(j + 1, n):
            factor[i, j] = mm(left[i, j], diag, 1, 0)
        z = eps[:, spans[j]]
        for k in range(j):
            z = z - mm(solved[k][0], factor[j, k], 1, 1)
        solved.append((z, mm(z, diag, 1, 0)))
    xs = [w for _, w in solved]
    for i in reversed(range(n)):
        for j in range(i):
            xs[j] = xs[j] - mm(xs[i], factor[i, j], 1, 0)
    x = jnp.concatenate(xs, axis=1)
    x = x - jnp.sum(x, axis=1, keepdims=True) * inv
    size = jnp.sum(mm(x, gram[...], 1, 0) * x, axis=1, keepdims=True)
    clip = jnp.minimum(1.0, limit / jnp.sqrt(jnp.maximum(size, 0.0)))
    x_ref[...] = x * (clip * -(inv**0.5))


def solve(core, mine, other, limit):
    count, half = mine.shape
    samples = 2 * half
    return call(
        functools.partial(solve_kernel, limit),
        jax.ShapeDtypeStruct((8, samples), F32),
        pltpu.PrefetchScalarGridSpec(
            num_scalar_prefetch=1,
            grid=(1,),
            in_specs=[pl.BlockSpec((count, half), lambda i, s: (0, 0))] * 2,
            out_specs=pl.BlockSpec((8, samples), lambda i, s: (0, 0)),
            scratch_shapes=[
                pltpu.VMEM((2 * count, half), F32),
                pltpu.VMEM((samples, samples), F32),
            ],
        ),
        vmem=kernel_mib(half),
    )(core, mine, other)


def update_kernel(rows, place, x_ref, cn_ref, base_ref, *refs):
    far_refs, out_ref = refs[:-1], refs[-1]
    slabs, total, _ = cn_ref.shape
    sub = lax.broadcasted_iota(jnp.int32, (8, total), 0)

    def split(x):
        first = x.astype(BF16).astype(F32)
        rest = x - first
        second = rest.astype(BF16).astype(F32)
        x = jnp.where(sub == 0, first, jnp.where(sub == 1, second, rest - second))
        return jnp.where(sub < 3, x, 0.0).astype(BF16)

    low, high = x_ref[:, :total], x_ref[:, total:]
    is_low = place[0] == 0
    near = jnp.where(is_low, low, high)
    far = by_distance(jnp.where(is_low, high, low), 1, rows, place[2])
    weight = jnp.sum(far[:1], axis=1, keepdims=True)
    both = jnp.concatenate([split(near), split(far)], axis=1)

    def one(slab):
        span = slice(slab * rows, (slab + 1) * rows)
        block = jnp.concatenate([cn_ref[slab]] + [ref[span, :] for ref in far_refs], axis=0)
        y = jnp.dot(both, block, preferred_element_type=F32)
        out_ref[slab : slab + 1, :] = jnp.sum(y, axis=0, keepdims=True) - weight * base_ref[slab]

    for slab in range(slabs):
        one(slab)


def update(x, place, cn, base, far_blocks):
    slabs, total, width = cn.shape
    whole = pl.BlockSpec(memory_space=pltpu.VMEM)
    return call(
        functools.partial(update_kernel, total // len(far_blocks)),
        jax.ShapeDtypeStruct((slabs, width), F32),
        pltpu.PrefetchScalarGridSpec(
            num_scalar_prefetch=1,
            grid=(),
            in_specs=[whole] * (3 + len(far_blocks)),
            out_specs=whole,
        ),
        vmem=kernel_mib(total),
    )(place, x, cn, base, *far_blocks)


def xor_pairs(size, bits):
    return [(i, i ^ bits) for i in range(size)]


def sum_all(mine, other, parts):
    mine = mine + lax.ppermute(other, "col", SWAP)
    mine = mine + lax.ppermute(mine, "slab", SWAP)
    bit = 1
    while bit < parts:
        mine = mine + lax.ppermute(mine, "smp", xor_pairs(parts, bit))
        bit *= 2
    return mine, lax.ppermute(mine, "col", SWAP)


def shards(parts, slab_parts, col_parts, jacobian, local_energy):
    rows, slabs, columns = jacobian.shape
    params = slabs * slab_parts * columns * col_parts
    half = rows * parts // 2
    me = lax.axis_index("smp")
    count = parts // 2
    far = list(range(count, parts))
    high = me // count

    far_rows, after = [], jacobian
    group = max(1, count // 2)
    for k in range(0, count, group):
        far_rows += pack(after, parts, far[k : k + group])
        after, _ = lax.optimization_barrier((after, far_rows[-1]))
    (near_rows,) = pack(after, parts, [])
    near = lax.all_to_all(
        near_rows,
        "smp",
        split_axis=0,
        concat_axis=0,
        axis_index_groups=[list(range(count)), far],
        tiled=True,
    )
    far_blocks = [lax.ppermute(r, "smp", xor_pairs(parts, k)) for k, r in zip(far, far_rows)]

    extra = energy_rows(local_energy, parts)
    cn, base, near_gram = near_products(near, slabs)
    core = lax.axis_index("col")
    place = jnp.stack([high, core, me % count])
    mine, other = far_products(far_blocks, place, cn, base, near_gram, extra)
    mine, other = sum_all(mine, other, parts)
    x = solve(core[None], mine, other, 0.3 * float(params) ** 0.5)
    return update(x, place, cn, base, far_blocks)


def solution(mesh):
    body = functools.partial(shards, mesh.shape["smp"], mesh.shape["slab"], mesh.shape["col"])
    in_specs = (P("smp", "slab", "col"), P("smp"))
    out_specs = P("slab", ("col", "smp"))
    return jax.shard_map(body, mesh=mesh, in_specs=in_specs, out_specs=out_specs, check_vma=False)
```

```python
import functools

import jax
import jax.numpy as jnp
from jax import lax
from jax.experimental import pallas as pl
from jax.experimental.pallas import tpu as pltpu
from jax.sharding import PartitionSpec as P

BLOCK = 64
LANES = 128
EXTRA = 16
TRANSFER_FLOPS = 10**11
CHUNK = 256
F32 = jnp.float32
BF16 = jnp.bfloat16
HIGHEST = lax.Precision.HIGHEST
MIB = 1024 * 1024
SWAP = [(0, 1), (1, 0)]


def mm(a, b, ca, cb):
    return lax.dot_general(
        a, b, (((ca,), (cb,)), ((), ())), precision=HIGHEST, preferred_element_type=F32
    )


def products(a, b):
    return lax.dot_general(a, b, (((1,), (1,)), ((), ())), preferred_element_type=F32)


def call(kernel, out_shape, grid_spec=None, vmem=58, flops=0, **kw):
    if grid_spec is not None:
        kw["grid_spec"] = grid_spec
    return pl.pallas_call(
        kernel,
        out_shape=out_shape,
        compiler_params=pltpu.CompilerParams(vmem_limit_bytes=vmem * MIB),
        cost_estimate=pl.CostEstimate(flops=flops, bytes_accessed=0, transcendentals=0),
        **kw,
    )


def kernel_mib(half):
    return 16 if half <= 128 else 40


def lane_chunks(width):
    size = min(CHUNK, width)
    return [slice(c, c + size) for c in range(0, width, size)]


def pack_kernel(parts, far, j_ref, *refs):
    half = parts // 2
    out_refs, (buffer, out, in_sems, out_sems) = refs[:-4], refs[-4:]
    count, rows, slabs, width = buffer.shape
    me = lax.axis_index("smp")

    def read(k):
        dest = me ^ far[k] if far else me // half * half + k
        columns = pl.ds(pl.multiple_of(dest * width, LANES), width)
        return pltpu.make_async_copy(j_ref.at[:, :, columns], buffer.at[k], in_sems.at[k])

    def write(k):
        target = out_refs[k] if far else out_refs[0].at[k]
        return pltpu.make_async_copy(out.at[k], target, out_sems.at[k])

    for k in range(count):
        read(k).start()
    for k in range(count):
        read(k).wait()
        for part in lane_chunks(width):
            x = jnp.swapaxes(buffer[k, :, :, part].astype(F32), 0, 1)
            out[k, :, part] = x.reshape(slabs * rows, x.shape[2]).astype(BF16)
        write(k).start()
    for k in range(count):
        write(k).wait()


def pack(jacobian, parts, far):
    rows, slabs, columns = jacobian.shape
    count, width = len(far) or parts // 2, columns // parts
    height = slabs * rows
    shapes = [(height, width)] * count if far else [(count, height, width)]
    return call(
        functools.partial(pack_kernel, parts, far),
        [pltpu.HBM(shape, BF16) for shape in shapes],
        pl.GridSpec(
            grid=(),
            in_specs=[pl.BlockSpec(memory_space=pl.ANY)],
            out_specs=[pl.BlockSpec(memory_space=pl.ANY)] * len(shapes),
            scratch_shapes=[
                pltpu.VMEM((count, rows, slabs, width), BF16),
                pltpu.VMEM((count, height, width), BF16),
                pltpu.SemaphoreType.DMA((count,)),
                pltpu.SemaphoreType.DMA((count,)),
            ],
        ),
        vmem=58,
    )(jacobian)


def near_kernel(rows, near_ref, c_ref, base_ref, gram_ref):
    step = pl.program_id(0)
    parts, height, width = near_ref.shape
    total = parts * rows

    @pl.when(step == 0)
    def _():
        gram_ref[...] = jnp.zeros_like(gram_ref)

    for half in range(height // rows):
        slab = pl.ds(half * rows, rows)
        for part in lane_chunks(width):
            sums = 0.0
            for k in range(parts):
                sums = sums + jnp.sum(near_ref[k, slab, part].astype(F32), axis=0, keepdims=True)
            base = sums * (1.0 / total)
            base_ref[half, :, part] = base
            for k in range(parts):
                x = near_ref[k, slab, part].astype(F32) - base
                c_ref[half, k * rows : (k + 1) * rows, part] = x.astype(BF16)
        c = c_ref[half]
        gram_ref[...] += products(c, c)


def near_products(near, slabs):
    parts, height, width = near.shape
    rows = height // slabs
    total = parts * rows
    group = 2
    return call(
        functools.partial(near_kernel, rows),
        (
            jax.ShapeDtypeStruct((slabs, total, width), BF16),
            jax.ShapeDtypeStruct((slabs, 1, width), F32),
            jax.ShapeDtypeStruct((total, total), F32),
        ),
        pl.GridSpec(
            grid=(slabs // group,),
            in_specs=[pl.BlockSpec((parts, group * rows, width), lambda i: (0, i, 0))],
            out_specs=[
                pl.BlockSpec((group, total, width), lambda i: (i, 0, 0)),
                pl.BlockSpec((group, 1, width), lambda i: (i, 0, 0)),
                pl.BlockSpec((total, total), lambda i: (0, 0)),
            ],
        ),
        vmem=kernel_mib(total),
    )(near)


def by_distance(x, axis, size, place):
    blocks = x.shape[axis] // size
    bit = 1
    while bit < blocks:
        parts = [lax.slice_in_dim(x, size * (i ^ bit), size * ((i ^ bit) + 1), axis=axis) for i in range(blocks)]
        x = jnp.where((place & bit) > 0, jnp.concatenate(parts, axis=axis), x)
        bit *= 2
    return x


def far_kernel(rows, place, *refs):
    far_refs, (cn_ref, base_ref, near_ref, extra_ref, mine_ref, other_ref, last_ref, gram, far) = refs[:-9], refs[-9:]
    slabs, total, width = cn_ref.shape

    def add(slab):
        span = slice(slab * rows, (slab + 1) * rows)
        for part in lane_chunks(width):
            base = base_ref[slab, :, part]
            for k, ref in enumerate(far_refs):
                x = ref[span, part].astype(F32) - base
                far[k * rows : (k + 1) * rows, part] = x.astype(BF16)
        last_ref[span, :] = far_refs[-1][span, :]
        c = far[...]
        return products(jnp.concatenate([cn_ref[slab], c], axis=0), c)

    total_products = add(0)
    for slab in range(1, slabs):
        total_products = total_products + add(slab)
    low = place[0] == 0
    products_far = by_distance(total_products, 1, rows, place[2])
    cross, far_far = products_far[:total], by_distance(products_far[total:], 0, rows, place[2])
    near_near = near_ref[...]
    low_low = jnp.where(low, near_near, far_far)
    high_high = jnp.where(low, far_far, near_near)
    row = lax.broadcasted_iota(jnp.int32, (total, total), 0)
    lane = lax.broadcasted_iota(jnp.int32, (total, total), 1)
    gram[:total, :] = jnp.where(row >= lane, low_low, high_high)
    gram[total : 2 * total, :] = jnp.where(low, cross, cross.T)
    diagonal = jnp.sum(jnp.where(row == lane, high_high, 0.0), axis=0, keepdims=True)
    gram[2 * total :, :] = jnp.where(row[:EXTRA] == 2, diagonal, extra_ref[...])
    count = mine_ref.shape[0]
    mine_ref[...] = gram[pl.ds(pl.multiple_of(place[1] * count, 8), count), :]
    other_ref[...] = gram[pl.ds(pl.multiple_of((1 - place[1]) * count, 8), count), :]


def far_products(far_blocks, place, cn, base, near_gram, extra):
    _, total, width = cn.shape
    rows = total // len(far_blocks)
    height = 2 * total + EXTRA
    share = jax.ShapeDtypeStruct((height // 2, total), F32)
    whole = pl.BlockSpec(memory_space=pltpu.VMEM)
    return call(
        functools.partial(far_kernel, rows),
        (share, share, pltpu.VMEM(far_blocks[-1].shape, BF16)),
        pltpu.PrefetchScalarGridSpec(
            num_scalar_prefetch=1,
            grid=(),
            in_specs=[whole] * (len(far_blocks) + 4),
            out_specs=[whole] * 3,
            scratch_shapes=[
                pltpu.VMEM((height, total), F32),
                pltpu.VMEM((total, width), BF16),
            ],
        ),
        vmem=kernel_mib(total),
    )(place, *far_blocks, cn, base, near_gram, extra)


def energy_kernel(parts, e_ref, out_ref):
    rows = e_ref.shape[1]
    me = lax.axis_index("smp")
    count = parts // 2
    lead = jnp.logical_and(lax.axis_index("col") == 0, lax.axis_index("slab") == 0)
    shape = out_ref.shape
    wide = jnp.concatenate([e_ref[...]] * count, axis=1)
    row = lax.broadcasted_iota(jnp.int32, shape, 0)
    block = lax.broadcasted_iota(jnp.int32, shape, 1) // rows
    mine = jnp.logical_and(row == me // count, block == me % count)
    out_ref[...] = jnp.where(jnp.logical_and(mine, lead), jnp.broadcast_to(wide, shape), 0.0)


def energy_rows(local_energy, parts):
    rows = local_energy.shape[0]
    return call(
        functools.partial(energy_kernel, parts),
        jax.ShapeDtypeStruct((EXTRA, rows * parts // 2), F32),
        vmem=16,
        flops=TRANSFER_FLOPS,
    )(local_energy[None])


def inverse(block):
    size = block.shape[0]
    shape = (8, 2 * size)
    lane = lax.broadcasted_iota(jnp.int32, shape, 1)
    sub = lax.broadcasted_iota(jnp.int32, shape, 0)
    wide = jnp.concatenate([block, jnp.zeros_like(block)], axis=1)
    count = size // 8
    tiles = [
        wide[8 * t : 8 * t + 8] + jnp.where(lane - size == sub + 8 * t, 1.0, 0.0) for t in range(count)
    ]
    scaled = []
    for t in range(count):
        normal = jnp.zeros(shape, F32)
        live = tiles[t:]
        cols = [[jnp.broadcast_to(x[:, 8 * t + j : 8 * t + j + 1], shape) for x in live] for j in range(8)]
        for at in range(0, 8, 2):
            c0, c1 = cols[at], cols[at + 1]
            a, b, c = c0[0][at : at + 1], c1[0][at : at + 1], c1[0][at + 1 : at + 2]
            d = 1.0 / (a * c - b * b)
            g0 = [(x * c - y * b) * d for x, y in zip(c0, c1)]
            g1 = [(y * a - x * b) * d for x, y in zip(c0, c1)]
            g0[0] = jnp.where(sub > at + 1, g0[0], 0.0)
            g1[0] = jnp.where(sub > at + 1, g1[0], 0.0)
            for j in range(at + 2, 8):
                u0, u1 = cols[j][0][at : at + 1], cols[j][0][at + 1 : at + 2]
                cols[j] = [x - (y * u0 + z * u1) for x, y, z in zip(cols[j], g0, g1)]
            r0, r1 = live[0][at : at + 1], live[0][at + 1 : at + 2]
            live = [x - (y * r0 + z * r1) for x, y, z in zip(live, g0, g1)]
            normal = jnp.where(sub == at, (r0 * c - r1 * b) * d, normal)
            normal = jnp.where(sub == at + 1, (r1 * a - r0 * b) * d, normal)
        tiles[t:] = live
        scaled.append(normal)
    w = jnp.concatenate(tiles, axis=0)[:, size:]
    n = jnp.concatenate(scaled, axis=0)[:, size:]
    return mm(w, n, 0, 0)


def solve_kernel(limit, core, mine_ref, other_ref, x_ref, sums, gram):
    count = mine_ref.shape[0]
    sums[pl.ds(pl.multiple_of(core[0] * count, 8), count), :] = mine_ref[...]
    sums[pl.ds(pl.multiple_of((1 - core[0]) * count, 8), count), :] = other_ref[...]
    half = sums.shape[1]
    samples = 2 * half
    both, cross = sums[:half, :], sums[half : 2 * half, :]
    e = sums[2 * half : 2 * half + 8, :]
    flipped, turned = both.T, cross.T
    row = lax.broadcasted_iota(jnp.int32, (half, half), 0)
    lane = lax.broadcasted_iota(jnp.int32, (half, half), 1)
    low = jnp.where(row >= lane, both, flipped)
    high = jnp.where(row < lane, both, jnp.where(row > lane, flipped, e[2:3]))
    inv = 1.0 / samples
    col_low = (jnp.sum(low, axis=1, keepdims=True) + jnp.sum(cross, axis=1, keepdims=True)) * inv
    col_high = (jnp.sum(high, axis=1, keepdims=True) + jnp.sum(turned, axis=1, keepdims=True)) * inv
    row_low = (jnp.sum(low, axis=0, keepdims=True) + jnp.sum(turned, axis=0, keepdims=True)) * inv
    row_high = (jnp.sum(high, axis=0, keepdims=True) + jnp.sum(cross, axis=0, keepdims=True)) * inv
    mean = (jnp.sum(row_low, axis=1, keepdims=True) + jnp.sum(row_high, axis=1, keepdims=True)) * inv
    gram[:half, :half] = (low - col_low - row_low + mean) * inv
    gram[half:, half:] = (high - col_high - row_high + mean) * inv
    gram[half:, :half] = (turned - col_high - row_low + mean) * inv
    gram[:half, half:] = (cross - col_low - row_high + mean) * inv
    n = samples // BLOCK
    spans = [slice(BLOCK * i, BLOCK * (i + 1)) for i in range(n)]
    on = lax.broadcasted_iota(jnp.int32, (BLOCK, BLOCK), 0) == lax.broadcasted_iota(
        jnp.int32, (BLOCK, BLOCK), 1
    )
    diagonal = sum(jnp.where(on, gram[s, s], 0.0) for s in spans)
    diagonal = jnp.sum(diagonal, axis=0, keepdims=True)
    shift = jnp.sum(diagonal, axis=1, keepdims=True) * (0.01 * inv)

    energies = jnp.concatenate([e[0:1], e[1:2]], axis=1)
    center = jnp.sum(energies, axis=1, keepdims=True) * inv
    eps = jnp.broadcast_to((energies - center) * (inv**0.5), (8, samples))

    left, factor, solved = {}, {}, []
    for j in range(n):
        for i in range(j, n):
            block = gram[spans[i], spans[j]]
            if i == j:
                block = jnp.where(on, block + shift, block)
            for k in range(j):
                block = block - mm(factor[i, k], left[j, k], 1, 1)
            left[i, j] = block
        diag = inverse(left[j, j])
        for i in range(j + 1, n):
            factor[i, j] = mm(left[i, j], diag, 1, 0)
        z = eps[:, spans[j]]
        for k in range(j):
            z = z - mm(solved[k][0], factor[j, k], 1, 1)
        solved.append((z, mm(z, diag, 1, 0)))
    xs = [w for _, w in solved]
    for i in reversed(range(n)):
        for j in range(i):
            xs[j] = xs[j] - mm(xs[i], factor[i, j], 1, 0)
    x = jnp.concatenate(xs, axis=1)
    x = x - jnp.sum(x, axis=1, keepdims=True) * inv
    size = jnp.sum(mm(x, gram[...], 1, 0) * x, axis=1, keepdims=True)
    clip = jnp.minimum(1.0, limit / jnp.sqrt(jnp.maximum(size, 0.0)))
    x_ref[...] = x * (clip * -(inv**0.5))


def solve(core, mine, other, limit):
    count, half = mine.shape
    samples = 2 * half
    return call(
        functools.partial(solve_kernel, limit),
        jax.ShapeDtypeStruct((8, samples), F32),
        pltpu.PrefetchScalarGridSpec(
            num_scalar_prefetch=1,
            grid=(1,),
            in_specs=[pl.BlockSpec((count, half), lambda i, s: (0, 0))] * 2,
            out_specs=pl.BlockSpec((8, samples), lambda i, s: (0, 0)),
            scratch_shapes=[
                pltpu.VMEM((2 * count, half), F32),
                pltpu.VMEM((samples, samples), F32),
            ],
        ),
        vmem=kernel_mib(half),
    )(core, mine, other)


def update_kernel(rows, place, x_ref, cn_ref, base_ref, *refs):
    far_refs, out_ref = refs[:-1], refs[-1]
    slabs, total, _ = cn_ref.shape
    sub = lax.broadcasted_iota(jnp.int32, (8, total), 0)

    def split(x):
        first = x.astype(BF16).astype(F32)
        rest = x - first
        second = rest.astype(BF16).astype(F32)
        x = jnp.where(sub == 0, first, jnp.where(sub == 1, second, rest - second))
        return jnp.where(sub < 3, x, 0.0).astype(BF16)

    low, high = x_ref[:, :total], x_ref[:, total:]
    is_low = place[0] == 0
    near = jnp.where(is_low, low, high)
    far = by_distance(jnp.where(is_low, high, low), 1, rows, place[2])
    weight = jnp.sum(far[:1], axis=1, keepdims=True)
    both = jnp.concatenate([split(near), split(far)], axis=1)

    def one(slab):
        span = slice(slab * rows, (slab + 1) * rows)
        block = jnp.concatenate([cn_ref[slab]] + [ref[span, :] for ref in far_refs], axis=0)
        y = jnp.dot(both, block, preferred_element_type=F32)
        out_ref[slab : slab + 1, :] = jnp.sum(y, axis=0, keepdims=True) - weight * base_ref[slab]

    for slab in range(slabs):
        one(slab)


def update(x, place, cn, base, far_blocks):
    slabs, total, width = cn.shape
    whole = pl.BlockSpec(memory_space=pltpu.VMEM)
    return call(
        functools.partial(update_kernel, total // len(far_blocks)),
        jax.ShapeDtypeStruct((slabs, width), F32),
        pltpu.PrefetchScalarGridSpec(
            num_scalar_prefetch=1,
            grid=(),
            in_specs=[whole] * (3 + len(far_blocks)),
            out_specs=whole,
        ),
        vmem=kernel_mib(total),
    )(place, x, cn, base, *far_blocks)


def xor_pairs(size, bits):
    return [(i, i ^ bits) for i in range(size)]


def sum_all(mine, other, parts):
    mine = mine + lax.ppermute(other, "col", SWAP)
    mine = mine + lax.ppermute(mine, "slab", SWAP)
    bit = 1
    while bit < parts:
        mine = mine + lax.ppermute(mine, "smp", xor_pairs(parts, bit))
        bit *= 2
    return mine, lax.ppermute(mine, "col", SWAP)


def shards(parts, slab_parts, col_parts, jacobian, local_energy):
    rows, slabs, columns = jacobian.shape
    params = slabs * slab_parts * columns * col_parts
    half = rows * parts // 2
    me = lax.axis_index("smp")
    count = parts // 2
    far = list(range(count, parts))
    high = me // count

    far_rows, after = [], jacobian
    group = max(1, count // 2)
    for k in range(0, count, group):
        far_rows += pack(after, parts, far[k : k + group])
        after, _ = lax.optimization_barrier((after, far_rows[-1]))
    (near_rows,) = pack(after, parts, [])
    near = lax.all_to_all(
        near_rows,
        "smp",
        split_axis=0,
        concat_axis=0,
        axis_index_groups=[list(range(count)), far],
        tiled=True,
    )
    far_blocks = [lax.ppermute(r, "smp", xor_pairs(parts, k)) for k, r in zip(far, far_rows)]

    extra = energy_rows(local_energy, parts)
    cn, base, near_gram = near_products(near, slabs)
    core = lax.axis_index("col")
    place = jnp.stack([high, core, me % count])
    mine, other, last = far_products(far_blocks, place, cn, base, near_gram, extra)
    mine, other = sum_all(mine, other, parts)
    x = solve(core[None], mine, other, 0.3 * float(params) ** 0.5)
    return update(x, place, cn, base, [*far_blocks[:-1], last])


def solution(mesh):
    body = functools.partial(shards, mesh.shape["smp"], mesh.shape["slab"], mesh.shape["col"])
    in_specs = (P("smp", "slab", "col"), P("smp"))
    out_specs = P("slab", ("col", "smp"))
    return jax.shard_map(body, mesh=mesh, in_specs=in_specs, out_specs=out_specs, check_vma=False)
```

```python
import functools

import jax
import jax.numpy as jnp
from jax import lax
from jax.experimental import pallas as pl
from jax.experimental.pallas import tpu as pltpu
from jax.sharding import PartitionSpec as P

BLOCK = 64
LANES = 128
EXTRA = 16
TRANSFER_FLOPS = 10**11
CHUNK = 256
F32 = jnp.float32
BF16 = jnp.bfloat16
HIGHEST = lax.Precision.HIGHEST
MIB = 1024 * 1024
SWAP = [(0, 1), (1, 0)]


def mm(a, b, ca, cb):
    return lax.dot_general(
        a, b, (((ca,), (cb,)), ((), ())), precision=HIGHEST, preferred_element_type=F32
    )


def products(a, b):
    return lax.dot_general(a, b, (((1,), (1,)), ((), ())), preferred_element_type=F32)


def call(kernel, out_shape, grid_spec=None, vmem=58, flops=0, **kw):
    if grid_spec is not None:
        kw["grid_spec"] = grid_spec
    return pl.pallas_call(
        kernel,
        out_shape=out_shape,
        compiler_params=pltpu.CompilerParams(vmem_limit_bytes=vmem * MIB),
        cost_estimate=pl.CostEstimate(flops=flops, bytes_accessed=0, transcendentals=0),
        **kw,
    )


def kernel_mib(half):
    return 16 if half <= 128 else 40


def lane_chunks(width):
    size = min(CHUNK, width)
    return [slice(c, c + size) for c in range(0, width, size)]


def pack_kernel(parts, far, j_ref, *refs):
    half = parts // 2
    out_refs, (buffer, out, in_sems, out_sems) = refs[:-4], refs[-4:]
    count, rows, slabs, width = buffer.shape
    me = lax.axis_index("smp")

    def read(k):
        dest = me ^ far[k] if far else me // half * half + k
        columns = pl.ds(pl.multiple_of(dest * width, LANES), width)
        return pltpu.make_async_copy(j_ref.at[:, :, columns], buffer.at[k], in_sems.at[k])

    def write(k):
        target = out_refs[k] if far else out_refs[0].at[k]
        return pltpu.make_async_copy(out.at[k], target, out_sems.at[k])

    for k in range(count):
        read(k).start()
    for k in range(count):
        read(k).wait()
        for part in lane_chunks(width):
            x = jnp.swapaxes(buffer[k, :, :, part].astype(F32), 0, 1)
            out[k, :, part] = x.reshape(slabs * rows, x.shape[2]).astype(BF16)
        write(k).start()
    for k in range(count):
        write(k).wait()


def pack(jacobian, parts, far):
    rows, slabs, columns = jacobian.shape
    count, width = len(far) or parts // 2, columns // parts
    height = slabs * rows
    shapes = [(height, width)] * count if far else [(count, height, width)]
    return call(
        functools.partial(pack_kernel, parts, far),
        [pltpu.HBM(shape, BF16) for shape in shapes],
        pl.GridSpec(
            grid=(),
            in_specs=[pl.BlockSpec(memory_space=pl.ANY)],
            out_specs=[pl.BlockSpec(memory_space=pl.ANY)] * len(shapes),
            scratch_shapes=[
                pltpu.VMEM((count, rows, slabs, width), BF16),
                pltpu.VMEM((count, height, width), BF16),
                pltpu.SemaphoreType.DMA((count,)),
                pltpu.SemaphoreType.DMA((count,)),
            ],
        ),
        vmem=58,
    )(jacobian)


def near_kernel(rows, near_ref, c_ref, base_ref, gram_ref):
    step = pl.program_id(0)
    parts, height, width = near_ref.shape
    total = parts * rows

    @pl.when(step == 0)
    def _():
        gram_ref[...] = jnp.zeros_like(gram_ref)

    for half in range(height // rows):
        slab = pl.ds(half * rows, rows)
        for part in lane_chunks(width):
            sums = 0.0
            for k in range(parts):
                sums = sums + jnp.sum(near_ref[k, slab, part].astype(F32), axis=0, keepdims=True)
            base = sums * (1.0 / total)
            base_ref[half, :, part] = base
            for k in range(parts):
                x = near_ref[k, slab, part].astype(F32) - base
                c_ref[half, k * rows : (k + 1) * rows, part] = x.astype(BF16)
        c = c_ref[half]
        gram_ref[...] += products(c, c)


def near_products(near, slabs):
    parts, height, width = near.shape
    rows = height // slabs
    total = parts * rows
    group = 2
    return call(
        functools.partial(near_kernel, rows),
        (
            jax.ShapeDtypeStruct((slabs, total, width), BF16),
            jax.ShapeDtypeStruct((slabs, 1, width), F32),
            jax.ShapeDtypeStruct((total, total), F32),
        ),
        pl.GridSpec(
            grid=(slabs // group,),
            in_specs=[pl.BlockSpec((parts, group * rows, width), lambda i: (0, i, 0))],
            out_specs=[
                pl.BlockSpec((group, total, width), lambda i: (i, 0, 0)),
                pl.BlockSpec((group, 1, width), lambda i: (i, 0, 0)),
                pl.BlockSpec((total, total), lambda i: (0, 0)),
            ],
        ),
        vmem=kernel_mib(total),
    )(near)


def by_distance(x, axis, size, place):
    blocks = x.shape[axis] // size
    bit = 1
    while bit < blocks:
        parts = [lax.slice_in_dim(x, size * (i ^ bit), size * ((i ^ bit) + 1), axis=axis) for i in range(blocks)]
        x = jnp.where((place & bit) > 0, jnp.concatenate(parts, axis=axis), x)
        bit *= 2
    return x


def far_kernel(rows, place, *refs):
    far_refs, (cn_ref, base_ref, near_ref, extra_ref, mine_ref, other_ref, last_ref, gram, far) = refs[:-9], refs[-9:]
    slabs, total, width = cn_ref.shape

    def add(slab):
        span = slice(slab * rows, (slab + 1) * rows)
        for part in lane_chunks(width):
            base = base_ref[slab, :, part]
            for k, ref in enumerate(far_refs):
                x = ref[span, part].astype(F32) - base
                far[k * rows : (k + 1) * rows, part] = x.astype(BF16)
        last_ref[span, :] = far_refs[-1][span, :]
        c = far[...]
        return products(jnp.concatenate([cn_ref[slab], c], axis=0), c)

    total_products = add(0)
    for slab in range(1, slabs):
        total_products = total_products + add(slab)
    low = place[0] == 0
    products_far = by_distance(total_products, 1, rows, place[2])
    cross, far_far = products_far[:total], by_distance(products_far[total:], 0, rows, place[2])
    near_near = near_ref[...]
    low_low = jnp.where(low, near_near, far_far)
    high_high = jnp.where(low, far_far, near_near)
    row = lax.broadcasted_iota(jnp.int32, (total, total), 0)
    lane = lax.broadcasted_iota(jnp.int32, (total, total), 1)
    gram[:total, :] = jnp.where(row >= lane, low_low, high_high)
    gram[total : 2 * total, :] = jnp.where(low, cross, cross.T)
    diagonal = jnp.sum(jnp.where(row == lane, high_high, 0.0), axis=0, keepdims=True)
    gram[2 * total :, :] = jnp.where(row[:EXTRA] == 2, diagonal, extra_ref[...])
    count = mine_ref.shape[0]
    mine_ref[...] = gram[pl.ds(pl.multiple_of(place[1] * count, 8), count), :]
    other_ref[...] = gram[pl.ds(pl.multiple_of((1 - place[1]) * count, 8), count), :]


def far_products(far_blocks, place, cn, base, near_gram, extra):
    _, total, width = cn.shape
    rows = total // len(far_blocks)
    height = 2 * total + EXTRA
    share = jax.ShapeDtypeStruct((height // 2, total), F32)
    whole = pl.BlockSpec(memory_space=pltpu.VMEM)
    return call(
        functools.partial(far_kernel, rows),
        (share, share, pltpu.VMEM(far_blocks[-1].shape, BF16)),
        pltpu.PrefetchScalarGridSpec(
            num_scalar_prefetch=1,
            grid=(),
            in_specs=[whole] * (len(far_blocks) + 4),
            out_specs=[whole] * 3,
            scratch_shapes=[
                pltpu.VMEM((height, total), F32),
                pltpu.VMEM((total, width), BF16),
            ],
        ),
        vmem=kernel_mib(total),
    )(place, *far_blocks, cn, base, near_gram, extra)


def energy_kernel(parts, e_ref, out_ref):
    rows = e_ref.shape[1]
    me = lax.axis_index("smp")
    count = parts // 2
    lead = jnp.logical_and(lax.axis_index("col") == 0, lax.axis_index("slab") == 0)
    shape = out_ref.shape
    wide = jnp.concatenate([e_ref[...]] * count, axis=1)
    row = lax.broadcasted_iota(jnp.int32, shape, 0)
    block = lax.broadcasted_iota(jnp.int32, shape, 1) // rows
    mine = jnp.logical_and(row == me // count, block == me % count)
    out_ref[...] = jnp.where(jnp.logical_and(mine, lead), jnp.broadcast_to(wide, shape), 0.0)


def energy_rows(local_energy, parts):
    rows = local_energy.shape[0]
    return call(
        functools.partial(energy_kernel, parts),
        jax.ShapeDtypeStruct((EXTRA, rows * parts // 2), F32),
        vmem=16,
        flops=TRANSFER_FLOPS,
    )(local_energy[None])


def inverse(block):
    size = block.shape[0]
    shape = (8, 2 * size)
    lane = lax.broadcasted_iota(jnp.int32, shape, 1)
    sub = lax.broadcasted_iota(jnp.int32, shape, 0)
    wide = jnp.concatenate([block, jnp.zeros_like(block)], axis=1)
    count = size // 8
    tiles = [
        wide[8 * t : 8 * t + 8] + jnp.where(lane - size == sub + 8 * t, 1.0, 0.0) for t in range(count)
    ]
    scaled = []
    for t in range(count):
        normal = jnp.zeros(shape, F32)
        live = tiles[t:]
        cols = [[jnp.broadcast_to(x[:, 8 * t + j : 8 * t + j + 1], shape) for x in live] for j in range(8)]
        for at in range(0, 8, 2):
            c0, c1 = cols[at], cols[at + 1]
            a, b, c = c0[0][at : at + 1], c1[0][at : at + 1], c1[0][at + 1 : at + 2]
            d = 1.0 / (a * c - b * b)
            g0 = [(x * c - y * b) * d for x, y in zip(c0, c1)]
            g1 = [(y * a - x * b) * d for x, y in zip(c0, c1)]
            g0[0] = jnp.where(sub > at + 1, g0[0], 0.0)
            g1[0] = jnp.where(sub > at + 1, g1[0], 0.0)
            for j in range(at + 2, 8):
                u0, u1 = cols[j][0][at : at + 1], cols[j][0][at + 1 : at + 2]
                cols[j] = [x - (y * u0 + z * u1) for x, y, z in zip(cols[j], g0, g1)]
            r0, r1 = live[0][at : at + 1], live[0][at + 1 : at + 2]
            live = [x - (y * r0 + z * r1) for x, y, z in zip(live, g0, g1)]
            normal = jnp.where(sub == at, (r0 * c - r1 * b) * d, normal)
            normal = jnp.where(sub == at + 1, (r1 * a - r0 * b) * d, normal)
        tiles[t:] = live
        scaled.append(normal)
    w = jnp.concatenate(tiles, axis=0)[:, size:]
    n = jnp.concatenate(scaled, axis=0)[:, size:]
    return mm(w, n, 0, 0)


def solve_kernel(limit, core, mine_ref, other_ref, x_ref, sums, gram):
    count = mine_ref.shape[0]
    sums[pl.ds(pl.multiple_of(core[0] * count, 8), count), :] = mine_ref[...]
    sums[pl.ds(pl.multiple_of((1 - core[0]) * count, 8), count), :] = other_ref[...]
    half = sums.shape[1]
    samples = 2 * half
    both, cross = sums[:half, :], sums[half : 2 * half, :]
    e = sums[2 * half : 2 * half + 8, :]
    flipped, turned = both.T, cross.T
    row = lax.broadcasted_iota(jnp.int32, (half, half), 0)
    lane = lax.broadcasted_iota(jnp.int32, (half, half), 1)
    low = jnp.where(row >= lane, both, flipped)
    high = jnp.where(row < lane, both, jnp.where(row > lane, flipped, e[2:3]))
    inv = 1.0 / samples
    col_low = (jnp.sum(low, axis=1, keepdims=True) + jnp.sum(cross, axis=1, keepdims=True)) * inv
    col_high = (jnp.sum(high, axis=1, keepdims=True) + jnp.sum(turned, axis=1, keepdims=True)) * inv
    row_low = (jnp.sum(low, axis=0, keepdims=True) + jnp.sum(turned, axis=0, keepdims=True)) * inv
    row_high = (jnp.sum(high, axis=0, keepdims=True) + jnp.sum(cross, axis=0, keepdims=True)) * inv
    mean = (jnp.sum(row_low, axis=1, keepdims=True) + jnp.sum(row_high, axis=1, keepdims=True)) * inv
    gram[:half, :half] = (low - col_low - row_low + mean) * inv
    gram[half:, half:] = (high - col_high - row_high + mean) * inv
    gram[half:, :half] = (turned - col_high - row_low + mean) * inv
    gram[:half, half:] = (cross - col_low - row_high + mean) * inv
    n = samples // BLOCK
    spans = [slice(BLOCK * i, BLOCK * (i + 1)) for i in range(n)]
    on = lax.broadcasted_iota(jnp.int32, (BLOCK, BLOCK), 0) == lax.broadcasted_iota(
        jnp.int32, (BLOCK, BLOCK), 1
    )
    diagonal = sum(jnp.where(on, gram[s, s], 0.0) for s in spans)
    diagonal = jnp.sum(diagonal, axis=0, keepdims=True)
    shift = jnp.sum(diagonal, axis=1, keepdims=True) * (0.01 * inv)

    energies = jnp.concatenate([e[0:1], e[1:2]], axis=1)
    center = jnp.sum(energies, axis=1, keepdims=True) * inv
    eps = jnp.broadcast_to((energies - center) * (inv**0.5), (8, samples))

    left, factor, solved = {}, {}, []
    for j in range(n):
        for i in range(j, n):
            block = gram[spans[i], spans[j]]
            if i == j:
                block = jnp.where(on, block + shift, block)
            for k in range(j):
                block = block - mm(factor[i, k], left[j, k], 1, 1)
            left[i, j] = block
        diag = inverse(left[j, j])
        for i in range(j + 1, n):
            factor[i, j] = mm(left[i, j], diag, 1, 0)
        z = eps[:, spans[j]]
        for k in range(j):
            z = z - mm(solved[k][0], factor[j, k], 1, 1)
        solved.append((z, mm(z, diag, 1, 0)))
    xs = [w for _, w in solved]
    for i in reversed(range(n)):
        for j in range(i):
            xs[j] = xs[j] - mm(xs[i], factor[i, j], 1, 0)
    x = jnp.concatenate(xs, axis=1)
    x = x - jnp.sum(x, axis=1, keepdims=True) * inv
    size = jnp.sum(mm(x, gram[...], 1, 0) * x, axis=1, keepdims=True)
    clip = jnp.minimum(1.0, limit / jnp.sqrt(jnp.maximum(size, 0.0)))
    x_ref[...] = x * (clip * -(inv**0.5))


def solve(core, mine, other, limit):
    count, half = mine.shape
    samples = 2 * half
    return call(
        functools.partial(solve_kernel, limit),
        jax.ShapeDtypeStruct((8, samples), F32),
        pltpu.PrefetchScalarGridSpec(
            num_scalar_prefetch=1,
            grid=(1,),
            in_specs=[pl.BlockSpec((count, half), lambda i, s: (0, 0))] * 2,
            out_specs=pl.BlockSpec((8, samples), lambda i, s: (0, 0)),
            scratch_shapes=[
                pltpu.VMEM((2 * count, half), F32),
                pltpu.VMEM((samples, samples), F32),
            ],
        ),
        vmem=kernel_mib(half),
    )(core, mine, other)


def update_kernel(rows, place, x_ref, cn_ref, base_ref, *refs):
    far_refs, out_ref = refs[:-1], refs[-1]
    slabs, total, _ = cn_ref.shape
    sub = lax.broadcasted_iota(jnp.int32, (8, total), 0)

    def split(x):
        first = x.astype(BF16).astype(F32)
        rest = x - first
        second = rest.astype(BF16).astype(F32)
        x = jnp.where(sub == 0, first, jnp.where(sub == 1, second, rest - second))
        return jnp.where(sub < 3, x, 0.0).astype(BF16)

    low, high = x_ref[:, :total], x_ref[:, total:]
    is_low = place[0] == 0
    near = jnp.where(is_low, low, high)
    far = by_distance(jnp.where(is_low, high, low), 1, rows, place[2])
    weight = jnp.sum(far[:1], axis=1, keepdims=True)
    both = jnp.concatenate([split(near), split(far)], axis=1)

    def one(slab):
        span = slice(slab * rows, (slab + 1) * rows)
        block = jnp.concatenate([cn_ref[slab]] + [ref[span, :] for ref in far_refs], axis=0)
        y = jnp.dot(both, block, preferred_element_type=F32)
        out_ref[slab : slab + 1, :] = jnp.sum(y, axis=0, keepdims=True) - weight * base_ref[slab]

    for slab in range(slabs):
        one(slab)


def update(x, place, cn, base, far_blocks):
    slabs, total, width = cn.shape
    whole = pl.BlockSpec(memory_space=pltpu.VMEM)
    return call(
        functools.partial(update_kernel, total // len(far_blocks)),
        jax.ShapeDtypeStruct((slabs, width), F32),
        pltpu.PrefetchScalarGridSpec(
            num_scalar_prefetch=1,
            grid=(),
            in_specs=[whole] * (3 + len(far_blocks)),
            out_specs=whole,
        ),
        vmem=kernel_mib(total),
    )(place, x, cn, base, *far_blocks)


def xor_pairs(size, bits):
    return [(i, i ^ bits) for i in range(size)]


def sum_all(mine, other, parts):
    mine = mine + lax.ppermute(other, "col", SWAP)
    b = lax.ppermute(mine, "slab", SWAP)
    c = lax.ppermute(mine, "smp", xor_pairs(parts, 1))
    d = lax.ppermute(
        mine, ("smp", "slab"), [(2 * i + j, 2 * (i ^ 1) + 1 - j) for i in range(parts) for j in range(2)]
    )
    mine = (mine + b) + (c + d)
    bit = 2
    while bit < parts:
        b = lax.ppermute(mine, "smp", xor_pairs(parts, bit))
        if 2 * bit < parts:
            c = lax.ppermute(mine, "smp", xor_pairs(parts, 2 * bit))
            d = lax.ppermute(mine, "smp", xor_pairs(parts, 3 * bit))
            mine = (mine + b) + (c + d)
        else:
            mine = mine + b
        bit *= 4
    return mine, lax.ppermute(mine, "col", SWAP)


def shards(parts, slab_parts, col_parts, jacobian, local_energy):
    rows, slabs, columns = jacobian.shape
    params = slabs * slab_parts * columns * col_parts
    half = rows * parts // 2
    me = lax.axis_index("smp")
    count = parts // 2
    far = list(range(count, parts))
    high = me // count

    far_rows, after = [], jacobian
    group = max(1, count // 2)
    for k in range(0, count, group):
        far_rows += pack(after, parts, far[k : k + group])
        after, _ = lax.optimization_barrier((after, far_rows[-1]))
    (near_rows,) = pack(after, parts, [])
    near = lax.all_to_all(
        near_rows,
        "smp",
        split_axis=0,
        concat_axis=0,
        axis_index_groups=[list(range(count)), far],
        tiled=True,
    )
    far_blocks = [lax.ppermute(r, "smp", xor_pairs(parts, k)) for k, r in zip(far, far_rows)]

    extra = energy_rows(local_energy, parts)
    cn, base, near_gram = near_products(near, slabs)
    core = lax.axis_index("col")
    place = jnp.stack([high, core, me % count])
    mine, other, last = far_products(far_blocks, place, cn, base, near_gram, extra)
    mine, other = sum_all(mine, other, parts)
    x = solve(core[None], mine, other, 0.3 * float(params) ** 0.5)
    return update(x, place, cn, base, [*far_blocks[:-1], last])


def solution(mesh):
    body = functools.partial(shards, mesh.shape["smp"], mesh.shape["slab"], mesh.shape["col"])
    in_specs = (P("smp", "slab", "col"), P("smp"))
    out_specs = P("slab", ("col", "smp"))
    return jax.shard_map(body, mesh=mesh, in_specs=in_specs, out_specs=out_specs, check_vma=False)
```
